256 devices in a mesh: dp: 8 (over x, z_hi), expert: 32 (over y, z_lo, core).
Axes of the slice: x: 4, y: 4, z: 8 (z_hi: 2, z_lo: 4; z = z_hi * 4 + z_lo), core: 2. Of those that a mesh axis runs over, the one named last changes fastest.
Arguments:
- tokens: bfloat16 [32768, 2048], P(('dp', 'expert')), may hold values from -6 to 6
- route_ids: int32 [32768, 2], P(('dp', 'expert')), may hold values from 0 to 31, all different within a row; in each aligned block of 128 rows (0 to 127, 128 to 255, ...) at most 16 rows name the same one
- route_gates: float32 [32768, 2], P(('dp', 'expert')), may hold values from 0.05 to 0.5
- cotangent: bfloat16 [32768, 2048], P(('dp', 'expert')), may hold values from -6 to 6
- old_owner: int32 [32], replicated, may hold values from 0 to 31, each once
- new_owner: int32 [32], replicated, may hold values from 0 to 31, each once
- weight_in: bfloat16 [32, 2048, 768], P('expert'), may hold values from -0.125 to 0.125
- weight_out: bfloat16 [32, 768, 2048], P('expert'), may hold values from -0.21875 to 0.21875
- mean_in: bfloat16 [32, 2048, 768], P('expert', 'dp'), may hold values from -3 to 3
- square_in: bfloat16 [32, 2048, 768], P('expert', 'dp'), may hold values from 0.099609375 to 2
- mean_out: bfloat16 [32, 768, 2048], P('expert', 'dp'), may hold values from -3 to 3
- square_out: bfloat16 [32, 768, 2048], P('expert', 'dp'), may hold values from 0.099609375 to 2
Outputs:
- mixed: bfloat16 [32768, 2048], P(('dp', 'expert'))
- new_weight_in: bfloat16 [32, 2048, 768], P('expert', 'dp')
- new_mean_in: bfloat16 [32, 2048, 768], P('expert', 'dp')
- new_square_in: bfloat16 [32, 2048, 768], P('expert', 'dp')
- new_weight_out: bfloat16 [32, 768, 2048], P('expert', 'dp')
- new_mean_out: bfloat16 [32, 768, 2048], P('expert', 'dp')
- new_square_out: bfloat16 [32, 768, 2048], P('expert', 'dp')
The draws below stay inside these ranges and needn't reach their ends.
Inputs may be any that keep to these rules, and one draw needn't show every extreme that they name: `route_ids`: each token names 2 different experts. The tokens of one device (aligned blocks of 128 tokens) name any one expert at most 16 times, a bound that some block reaches. `old_owner`: A permutation of the expert axis's indices. `new_owner`: A permutation of the expert axis's indices.
All inputs are finite; a program needn't handle non-finite values.
Results may differ from the reference program's by a relative error of at most 0.025.
Values may be sent and summed in bfloat16 or wider, within the bound.
A program may use at most 128 MiB of HBM per device.

```python
import math
import jax
import jax.numpy as jnp
import numpy as np
from jax import lax

D = 2048
F = 768
TOK_DEV = 128
TOPK = 2
EXPERTS = 32
CAP = 16
TOKENS = 32768
N_DP = 8
N_EXPERT = 32


def block_scale(stream_key, dims, cuts, smallest, top_value):
    factor_of, own = 1.0, jax.random.fold_in(stream_key, 6)
    for dim, parts in cuts:
        heights = jnp.exp(jax.random.uniform(jax.random.fold_in(own, dim), (parts,), jnp.float32, smallest / len(cuts), top_value / len(cuts)))
        factor_of = factor_of * jnp.repeat(heights, dims[dim] // parts).reshape([-1 if axis == dim else 1 for axis in range(len(dims))])
    return factor_of


def routed_block(key, own, number, rows, count, top, reach, skew):
    sequence = jax.random.permutation(key, count)
    heavy_load, ordinary = shares(count, rows * top, reach, skew, True), shares(count, rows * top, reach, skew, False)
    places = jnp.arange(count)

    def named(lengths, offset_by):
        used = int((lengths > 0).sum())
        fixed = max(1, used // 4)
        moved = fixed + (places - fixed + offset_by * (used - fixed)) % max(1, count - fixed)
        return jnp.zeros((count,), jnp.int32).at[sequence[jnp.where(places < fixed, places, moved)]].set(jnp.asarray(lengths, jnp.int32))

    lengths = jnp.where(number % 4 == 0, named(heavy_load, number // 4), named(ordinary, number - number // 4 - 1))
    mixed = jax.random.permutation(jax.random.fold_in(own, 3), count)
    giver, taker = mixed[0:count // 2 * 2:2], mixed[1:count // 2 * 2:2]
    slack = jnp.minimum(lengths[giver] - 1, reach - lengths[taker]) // 2
    slack = jnp.where((giver == sequence[0]) | (taker == sequence[0]) | (lengths[taker] == 0), 0, jnp.maximum(slack, 0))
    moved = jax.random.randint(jax.random.fold_in(own, 4), (count // 2,), 0, 1 << 20) % (slack + 1)
    lengths = lengths.at[giver].add(-moved).at[taker].add(moved)
    members = jnp.searchsorted(jnp.cumsum(lengths), jnp.arange(rows * top), side="right").astype(jnp.int32)
    table = members.reshape(top, rows).T
    table = table[jax.random.permutation(jax.random.fold_in(own, 1), rows)]
    offset_by = jax.random.randint(jax.random.fold_in(own, 2), (rows, 1), 0, top)
    return jnp.take_along_axis(table, (jnp.arange(top)[None, :] + offset_by) % top, axis=1)


def shares(number_of, total, limit, skew, full):
    weights = [(1 << 20) // math.isqrt(standing ** skew) + 1 for standing in range(1, number_of + 1)]
    largest = limit if full else min(limit, max(-(-total // number_of), total * weights[0] // sum(weights)))
    least = 1 if total - largest >= number_of - 1 else 0
    holding, rest = [largest] + [least] * (number_of - 1), total - largest - least * (number_of - 1)
    while rest > 0:
        candidates = [i for i in range(1, number_of) if holding[i] < largest] or [i for i in range(1, number_of) if holding[i] < limit]
        pool, budget = sum([weights[i] for i in candidates]), rest
        for i in candidates:
            addition = min(limit - holding[i], max(1, budget * weights[i] // pool), rest)
            holding[i] = holding[i] + addition
            rest = rest - addition
    return np.array(holding)


def scatter_about(stream_key, extent, width, limit, shards=(), held_as=jnp.bfloat16):
    drawn = jax.random.normal(stream_key, extent, jnp.float32) * width
    if len(shards) > 0:
        drawn = block_scale(stream_key, extent, shards, -0.22, 0.18) * drawn
    return jnp.clip(drawn, min=-limit, max=limit).astype(held_as)


def setup_inputs(seed: int = 0) -> dict:
    streams_of = jax.random.split(jax.random.key(seed), 13)
    tokens = scatter_about(streams_of[0], (TOKENS, D), 1.0, 6.0, ((0, 256),))
    route_ids_keys = jax.random.split(jax.random.fold_in(streams_of[1], 1), TOKENS // TOK_DEV)
    route_ids_turns = jax.random.permutation(jax.random.fold_in(streams_of[1], 3), TOKENS // TOK_DEV)
    route_ids = jax.vmap(lambda own, number: routed_block(jax.random.fold_in(streams_of[1], 2), own, number, TOK_DEV, EXPERTS, TOPK, CAP, 2))(route_ids_keys, route_ids_turns).reshape((TOKENS, TOPK))
    route_gates = jnp.clip(jnp.exp(math.log(0.5) - 2.3025851 * jax.random.uniform(streams_of[2], (TOKENS, TOPK), jnp.float32) ** block_scale(streams_of[2], (TOKENS, TOPK), ((0, 256),), -0.2, 0.2)), 0.05, 0.5)
    cotangent = scatter_about(streams_of[3], (TOKENS, D), 1.0, 6.0, ((0, 256),))
    old_owner = jax.random.permutation(streams_of[4], EXPERTS).astype(jnp.int32)
    new_owner = jax.random.permutation(streams_of[5], EXPERTS).astype(jnp.int32)
    weight_in = scatter_about(streams_of[6], (EXPERTS, D, F), D ** -0.5, 0.125, ((0, 32),))
    weight_out = scatter_about(streams_of[7], (EXPERTS, F, D), F ** -0.5, 0.21875, ((0, 32),))
    mean_in = scatter_about(streams_of[8], (EXPERTS, D, F), 0.5, 3.0, ((0, 32), (1, 8)))
    square_in = jnp.clip(jnp.exp(math.log(2.0) - 2.9996462 * jax.random.uniform(streams_of[9], (EXPERTS, D, F), jnp.float32) ** block_scale(streams_of[9], (EXPERTS, D, F), ((0, 32), (1, 8)), -0.2, 0.2)), 0.099609375, 2.0).astype(jnp.bfloat16)
    mean_out = scatter_about(streams_of[10], (EXPERTS, F, D), 0.5, 3.0, ((0, 32), (1, 8)))
    square_out = jnp.clip(jnp.exp(math.log(2.0) - 2.9996462 * jax.random.uniform(streams_of[11], (EXPERTS, F, D), jnp.float32) ** block_scale(streams_of[11], (EXPERTS, F, D), ((0, 32), (1, 8)), -0.2, 0.2)), 0.099609375, 2.0).astype(jnp.bfloat16)
    return dict(tokens=tokens, route_ids=route_ids, route_gates=route_gates, cotangent=cotangent, old_owner=old_owner, new_owner=new_owner, weight_in=weight_in, weight_out=weight_out, mean_in=mean_in, square_in=square_in, mean_out=mean_out, square_out=square_out)


beta_one = 0.9
beta_two = 0.95
adam_eps = 1e-08
learn_rate = 0.01
adam_step = 100.0

def silu_slope(preact):
    logistic = jax.nn.sigmoid(preact)
    return logistic * (1.0 + preact * (1.0 - logistic))

def adam_apply(weight, mean_old, square_old, gradient):
    mean_new = beta_one * mean_old.astype(jnp.float32) + (1.0 - beta_one) * gradient
    square_new = beta_two * square_old.astype(jnp.float32) + (1.0 - beta_two) * gradient * gradient
    stride = mean_new / (1.0 - beta_one ** adam_step) / (jnp.sqrt(square_new / (1.0 - beta_two ** adam_step)) + adam_eps)
    fresh = (weight.astype(jnp.float32) - learn_rate * stride).astype(jnp.bfloat16)
    return (fresh, mean_new.astype(jnp.bfloat16), square_new.astype(jnp.bfloat16))

def group_sum(partial_value):
    rounded = lax.optimization_barrier(partial_value.astype(jnp.bfloat16))
    return lax.optimization_barrier(jnp.sum(rounded.astype(jnp.float32), axis=0))

def reference(tokens, route_ids, route_gates, cotangent, old_owner, new_owner, weight_in, weight_out, mean_in, square_in, mean_out, square_out):
    experts_all = jnp.arange(EXPERTS, dtype=jnp.int32)
    picked = (route_ids[:, :, None] == experts_all[None, None, :]).astype(jnp.int32)
    counts = lax.optimization_barrier(jnp.sum(picked, axis=1)).reshape(-1, TOK_DEV, EXPERTS)
    before = (jnp.cumsum(counts, axis=1) - counts).reshape(TOKENS, EXPERTS)
    position = lax.optimization_barrier(jnp.sum(picked * before[:, None, :], axis=2)).astype(jnp.int32)
    token_ids = jnp.arange(TOKENS, dtype=jnp.int32)
    source = token_ids // TOK_DEV % N_EXPERT
    group_of = jnp.broadcast_to((token_ids // (TOK_DEV * N_EXPERT))[:, None], (TOKENS, TOPK)).astype(jnp.int32)
    slot = (source[:, None] * CAP + position).astype(jnp.int32)
    flat_row = (token_ids[:, None] * TOPK + jnp.arange(TOPK, dtype=jnp.int32)[None, :]).astype(jnp.int32)
    empty = TOKENS * TOPK
    table = jnp.full((N_DP, EXPERTS, N_EXPERT * CAP), empty, dtype=jnp.int32)
    table = table.at[group_of, route_ids, slot].set(flat_row)
    tokens_pad = jnp.concatenate([tokens, jnp.zeros((1, D), tokens.dtype)], axis=0)
    cotangent_pad = jnp.concatenate([cotangent, jnp.zeros((1, D), cotangent.dtype)], axis=0)
    gates_pad = jnp.concatenate([route_gates.reshape(-1), jnp.zeros((1,), route_gates.dtype)], axis=0)

    def one_expert(total, expert):
        entries = table[:, expert, :]
        token_of = jnp.where(entries < empty, entries // TOPK, TOKENS).astype(jnp.int32)
        gate_of = gates_pad[entries].astype(jnp.float32)
        inputs = tokens_pad[token_of].astype(jnp.float32)
        holder = old_owner[expert]
        upper = weight_in[holder]
        lower = weight_out[holder]
        preact = jnp.einsum('gsd,df->gsf', inputs, upper.astype(jnp.float32))
        hidden = jax.nn.silu(preact).astype(jnp.bfloat16)
        produced = jnp.einsum('gsf,fd->gsd', hidden.astype(jnp.float32), lower.astype(jnp.float32)).astype(jnp.bfloat16)
        total = total.at[token_of].add(gate_of[..., None] * produced.astype(jnp.float32))
        scaled = (gate_of[..., None] * cotangent_pad[token_of].astype(jnp.float32)).astype(jnp.bfloat16)
        downward = jnp.einsum('gsd,fd->gsf', scaled.astype(jnp.float32), lower.astype(jnp.float32))
        slope = (downward * silu_slope(preact)).astype(jnp.bfloat16)
        grad_in = group_sum(jnp.einsum('gsd,gsf->gdf', inputs, slope.astype(jnp.float32)))
        grad_out = group_sum(jnp.einsum('gsf,gsd->gfd', hidden.astype(jnp.float32), scaled.astype(jnp.float32)))
        updated_in = adam_apply(upper, mean_in[holder], square_in[holder], grad_in)
        updated_out = adam_apply(lower, mean_out[holder], square_out[holder], grad_out)
        return (total, updated_in + updated_out)
    total, stacked = lax.scan(one_expert, jnp.zeros((TOKENS + 1, D), jnp.float32), experts_all)
    mixed = total[:TOKENS].astype(jnp.bfloat16)
    placed = [jnp.zeros_like(piece).at[new_owner].set(piece) for piece in stacked]
    return (mixed, placed[0], placed[1], placed[2], placed[3], placed[4], placed[5])
```

```python
import jax
import jax.numpy as jnp
from jax import lax
from jax.sharding import PartitionSpec as P

beta_one = 0.9
beta_two = 0.95
adam_eps = 1e-08
learn_rate = 0.01
adam_step = 100.0


def silu_slope(preact):
    logistic = jax.nn.sigmoid(preact)
    return logistic * (1.0 + preact * (1.0 - logistic))


def adam_apply(weight, mean_old, square_old, gradient):
    mean_new = beta_one * mean_old.astype(jnp.float32) + (1.0 - beta_one) * gradient
    square_new = beta_two * square_old.astype(jnp.float32) + (1.0 - beta_two) * gradient * gradient
    stride = (
        mean_new
        / (1.0 - beta_one**adam_step)
        / (jnp.sqrt(square_new / (1.0 - beta_two**adam_step)) + adam_eps)
    )
    fresh = (weight.astype(jnp.float32) - learn_rate * stride).astype(jnp.bfloat16)
    return (fresh, mean_new.astype(jnp.bfloat16), square_new.astype(jnp.bfloat16))


def outer_dot(left, right):
    return lax.dot_general(
        left, right, (((0,), (0,)), ((), ())), preferred_element_type=jnp.float32
    )


def right_dot(left, right):
    return lax.dot_general(
        left, right, (((1,), (1,)), ((), ())), preferred_element_type=jnp.float32
    )


def body(
    tokens,
    route_ids,
    route_gates,
    cotangent,
    old_owner,
    new_owner,
    weight_in,
    weight_out,
    mean_in,
    square_in,
    mean_out,
    square_out,
):
    n_expert = lax.axis_size("expert")
    n_groups = lax.axis_size("dp")
    group = lax.axis_index("dp")
    tok_rows, width = tokens.shape
    picks_each = route_ids.shape[1]
    hidden_width = weight_in.shape[2]
    capacity = 2 * tok_rows * picks_each // n_expert
    slots_all = n_expert * capacity
    rows_in = width // n_groups
    rows_out = hidden_width // n_groups
    experts_all = jnp.arange(n_expert, dtype=jnp.int32)
    picked = (route_ids[:, :, None] == experts_all[None, None, :]).astype(jnp.int32)
    counts = jnp.sum(picked, axis=1)
    before = jnp.cumsum(counts, axis=0) - counts
    position = jnp.sum(picked * before[:, None, :], axis=2)
    slot = jnp.sum(picked * old_owner, axis=2) * capacity + position
    holder = (new_owner[:, None] == experts_all[None, :]).astype(jnp.int32)
    source_of = jnp.sum(holder * old_owner[:, None], axis=0)
    slot_ids = jnp.arange(slots_all, dtype=jnp.int32)
    place = [
        (slot[:, k][None, :] == slot_ids[:, None]).astype(jnp.bfloat16) for k in range(picks_each)
    ]

    def swap(rows):
        return lax.all_to_all(rows, "expert", split_axis=0, concat_axis=0, tiled=True)

    def exchange(rows):
        return swap(rows.reshape(n_expert, capacity, width)).reshape(slots_all, width)

    sent = jnp.dot(sum(place), tokens, preferred_element_type=jnp.float32).astype(jnp.bfloat16)
    arrived = exchange(sent)
    scaled = [
        (route_gates[:, k, None] * cotangent.astype(jnp.float32)).astype(jnp.bfloat16)
        for k in range(picks_each)
    ]
    graded = jnp.dot(
        jnp.concatenate(place, axis=1),
        jnp.concatenate(scaled, axis=0),
        preferred_element_type=jnp.float32,
    ).astype(jnp.bfloat16)
    upstream = exchange(graded)
    preact = jnp.dot(arrived, weight_in[0], preferred_element_type=jnp.float32)
    hidden = jax.nn.silu(preact).astype(jnp.bfloat16)
    produced = jnp.dot(hidden, weight_out[0], preferred_element_type=jnp.float32).astype(
        jnp.bfloat16
    )
    returned = exchange(produced)
    mixed = sum(
        route_gates[:, k, None] * outer_dot(place[k], returned) for k in range(picks_each)
    ).astype(jnp.bfloat16)
    downward = right_dot(upstream, weight_out[0])
    slope = (downward * silu_slope(preact)).astype(jnp.bfloat16)
    grad_out = lax.psum_scatter(
        outer_dot(hidden, upstream).astype(jnp.bfloat16), "dp", scatter_dimension=0, tiled=True
    ).astype(jnp.float32)
    grad_in = lax.psum_scatter(
        outer_dot(arrived, slope).astype(jnp.bfloat16), "dp", scatter_dimension=0, tiled=True
    ).astype(jnp.float32)
    in_share = lax.dynamic_slice_in_dim(weight_in[0], group * rows_in, rows_in, 0)
    out_share = lax.dynamic_slice_in_dim(weight_out[0], group * rows_out, rows_out, 0)
    after_in = adam_apply(in_share, mean_in[0], square_in[0], grad_in)
    after_out = adam_apply(out_share, mean_out[0], square_out[0], grad_out)
    lanes = 128
    deep = rows_in // n_expert
    wide = hidden_width // lanes
    tall = rows_out // 2
    cols = width // lanes

    def pieces_in(share):
        cut = share.reshape(n_expert, deep, wide, lanes).transpose(0, 2, 1, 3)
        return cut.reshape(n_expert, wide * deep, lanes)

    def joined_in(cut):
        share = cut.reshape(n_expert, wide, deep, lanes).transpose(0, 2, 1, 3)
        return share.reshape(1, rows_in, hidden_width)

    def pieces_out(share):
        cut = share.reshape(2, tall, cols, lanes).transpose(0, 2, 1, 3)
        return cut.reshape(n_expert, tall, lanes)

    def joined_out(cut):
        share = cut.reshape(2, cols, tall, lanes).transpose(0, 2, 1, 3)
        return share.reshape(1, rows_out, width)

    packed = jnp.concatenate(
        [pieces_in(part) for part in after_in] + [pieces_out(part) for part in after_out], axis=1
    )
    spread = swap(packed)
    landed = swap(jnp.take(spread, source_of, axis=0))
    moved = jnp.split(landed, 6, axis=1)
    return (
        mixed,
        joined_in(moved[0]),
        joined_in(moved[1]),
        joined_in(moved[2]),
        joined_out(moved[3]),
        joined_out(moved[4]),
        joined_out(moved[5]),
    )


def solution(mesh):
    return jax.shard_map(
        body,
        mesh=mesh,
        in_specs=(
            P(("dp", "expert"), None),
            P(("dp", "expert"), None),
            P(("dp", "expert"), None),
            P(("dp", "expert"), None),
            P(),
            P(),
            P("expert", None, None),
            P("expert", None, None),
            P("expert", "dp", None),
            P("expert", "dp", None),
            P("expert", "dp", None),
            P("expert", "dp", None),
        ),
        out_specs=(
            P(("dp", "expert"), None),
            P("expert", "dp", None),
            P("expert", "dp", None),
            P("expert", "dp", None),
            P("expert", "dp", None),
            P("expert", "dp", None),
            P("expert", "dp", None),
        ),
        check_vma=False,
    )
```

```python
import functools

import jax
import jax.numpy as jnp
from jax import lax
from jax.experimental import pallas as pl
from jax.experimental.pallas import tpu as pltpu
from jax.sharding import PartitionSpec as P

beta_one = 0.9
beta_two = 0.95
adam_eps = 1e-08
learn_rate = 0.01
adam_step = 100.0
n_ring = 4
n_half = 2
MESH = pl.DeviceIdType.MESH


def silu_slope(preact):
    logistic = jax.nn.sigmoid(preact)
    return logistic * (1.0 + preact * (1.0 - logistic))


def adam_apply(weight, mean_old, square_old, gradient):
    mean_new = beta_one * mean_old.astype(jnp.float32) + (1.0 - beta_one) * gradient
    square_new = beta_two * square_old.astype(jnp.float32) + (1.0 - beta_two) * gradient * gradient
    stride = (
        mean_new
        / (1.0 - beta_one**adam_step)
        / (jnp.sqrt(square_new / (1.0 - beta_two**adam_step)) + adam_eps)
    )
    fresh = (weight.astype(jnp.float32) - learn_rate * stride).astype(jnp.bfloat16)
    return (fresh, mean_new.astype(jnp.bfloat16), square_new.astype(jnp.bfloat16))


def outer_dot(left, right):
    return lax.dot_general(
        left, right, (((0,), (0,)), ((), ())), preferred_element_type=jnp.float32
    )


def right_dot(left, right):
    return lax.dot_general(
        left, right, (((1,), (1,)), ((), ())), preferred_element_type=jnp.float32
    )


def remote(src, dst, send, recv, device):
    return pltpu.make_async_remote_copy(
        src_ref=src, dst_ref=dst, send_sem=send, recv_sem=recv, device_id=device, device_id_type=MESH
    )


class Part:
    def __init__(self, rows, cols, piece):
        self.rows, self.cols, self.piece = rows, cols, piece
        self.share = rows // (n_ring * n_half)
        self.block = rows // n_ring
        self.side = cols // 2
        self.per_row = cols // piece[1]

    def where(self, i):
        r = pl.multiple_of((i // self.per_row) * self.piece[0], 16)
        c = pl.multiple_of((i % self.per_row) * self.piece[1], 128)
        return pl.ds(r, self.piece[0]), pl.ds(c, self.piece[1])

    def scratch(self, n_expert):
        half = (self.block, self.side)
        return dict(
            partial=pltpu.VMEM((self.rows, self.cols), jnp.bfloat16),
            landing=pltpu.VMEM((6,) + half, jnp.bfloat16),
            relayed=pltpu.VMEM((2,) + half, jnp.bfloat16),
            own=pltpu.VMEM((self.share, self.cols), jnp.float32),
            pair_out=pltpu.VMEM((self.share, self.cols), jnp.bfloat16),
            pair_in=pltpu.VMEM((self.share, self.cols), jnp.bfloat16),
            stage=pltpu.VMEM((n_expert, 3) + self.piece, jnp.bfloat16),
            hop_one=pltpu.VMEM((n_expert, 3) + self.piece, jnp.bfloat16),
            ordered=pltpu.VMEM((n_expert, 3) + self.piece, jnp.bfloat16),
            hop_two=pltpu.VMEM((n_expert, 3) + self.piece, jnp.bfloat16),
            ring_send=pltpu.SemaphoreType.DMA((6,)),
            ring_recv=pltpu.SemaphoreType.DMA((6,)),
            pair_send=pltpu.SemaphoreType.DMA,
            pair_recv=pltpu.SemaphoreType.DMA,
            one_send=pltpu.SemaphoreType.DMA((n_expert,)),
            one_recv=pltpu.SemaphoreType.DMA((n_expert,)),
            two_send=pltpu.SemaphoreType.DMA((n_expert,)),
            two_recv=pltpu.SemaphoreType.DMA((n_expert,)),
        )


part_names = tuple(Part(128, 256, (16, 128)).scratch(32))


class Refs:
    def __init__(self, names, refs):
        for name, ref in zip(names, refs):
            setattr(self, name, ref)


def finish_kernel(n_expert, parts, *refs):
    n_in = 18
    (
        source_of,
        slot,
        gates,
        produced,
        tok_t,
        slope,
        hid_t,
        upstream,
        w_in,
        m_in,
        s_in,
        w_out,
        m_out,
        s_out,
    ) = refs[:14]
    outs = refs[14:21]
    mixed = outs[0]
    returned, back_send, back_recv = refs[21:24]
    n = len(part_names)
    pin = Refs(part_names, refs[24 : 24 + n])
    pout = Refs(part_names, refs[24 + n : 24 + 2 * n])
    dp = lax.axis_index("dp")
    me = lax.axis_index("expert")
    x, zh = dp // 2, dp % 2
    ahead, behind, across = (x + 1) % 4, (x + 3) % 4, (x + 2) % 4
    to_ahead = (ahead * 2 + zh, me)
    to_behind = (behind * 2 + zh, me)
    to_pair = (x * 2 + 1 - zh, me)
    peers = n_expert - 1

    def peer(j):
        return (me + j) % n_expert

    barrier = pltpu.get_barrier_semaphore()

    @pl.loop(1, n_expert)
    def _(j):
        pl.semaphore_signal(barrier, inc=1, device_id=(dp, peer(j)), device_id_type=MESH)

    for device in (to_ahead, to_behind, to_pair):
        pl.semaphore_signal(barrier, inc=1, device_id=device, device_id_type=MESH)
    pl.semaphore_wait(barrier, peers + 3)

    def all_send(src, dst, send, recv):
        @pl.loop(1, n_expert)
        def _(j):
            d = peer(j)
            remote(src.at[d], dst.at[me], send.at[d], recv.at[me], (dp, d)).start()

        dst[me] = src[me]

    def all_recv(src, dst, send, recv):
        @pl.loop(1, n_expert)
        def _(j):
            d = peer(j)
            remote(src.at[d], dst.at[d], send.at[d], recv.at[d], (dp, d)).wait_recv()

    def all_sent(src, dst, send, recv):
        @pl.loop(1, n_expert)
        def _(j):
            d = peer(j)
            remote(src.at[d], dst.at[d], send.at[d], recv.at[d], (dp, d)).wait_send()

    def ring_copies(p, part):
        def side(block, half):
            r = pl.multiple_of(block * part.block, 16)
            return p.partial.at[pl.ds(r, part.block), pl.ds(half * part.side, part.side)]

        plan = [
            (side(across, 0), 0, to_ahead),
            (side(across, 1), 1, to_behind),
            (side(ahead, 1), 2, to_ahead),
            (side(behind, 0), 3, to_behind),
            (p.relayed.at[0], 4, to_ahead),
            (p.relayed.at[1], 5, to_behind),
        ]
        def copy(k):
            src, slot_of, device = plan[k]
            return remote(
                src, p.landing.at[slot_of], p.ring_send.at[k], p.ring_recv.at[k], device
            )

        return copy

    def ring_first(p, part, left, right):
        def fill(block):
            step = min(part.block, 256)
            base = block * part.block

            @pl.loop(0, part.block // step)
            def _(i):
                r = pl.ds(pl.multiple_of(base + i * step, 16), step)
                p.partial[r, :] = jnp.dot(
                    left[r, :], right[...], preferred_element_type=jnp.float32
                ).astype(jnp.bfloat16)

        copies = ring_copies(p, part)
        fill(across)
        copies(0).start()
        copies(1).start()
        fill(ahead)
        copies(2).start()
        fill(behind)
        copies(3).start()
        fill(x)

    def ring_second(p, part):
        copies = ring_copies(p, part)
        for k, block in ((0, ahead), (1, behind)):
            copies(k).wait_recv()

            @pl.loop(0, part.block // 16)
            def _(i):
                r = pl.ds(pl.multiple_of(i * 16, 16), 16)
                q = pl.ds(pl.multiple_of(block * part.block + i * 16, 16), 16)
                mine = p.partial[q, pl.ds(k * part.side, part.side)].astype(jnp.float32)
                p.relayed[k, r, :] = (p.landing[k, r, :].astype(jnp.float32) + mine).astype(
                    jnp.bfloat16
                )

            copies(4 + k).start()

    def pair_copy(p):
        return remote(p.pair_out, p.pair_in, p.pair_send, p.pair_recv, to_pair)

    def ring_third(p, part):
        copies = ring_copies(p, part)
        for k in (2, 3, 4, 5):
            copies(k).wait_recv()

        def total(half, base, i, k):
            r = pl.ds(pl.multiple_of(base + i * 16, 16), 16)
            q = pl.ds(pl.multiple_of(x * part.block + base + i * 16, 16), 16)
            mine = p.partial[q, pl.ds(half * part.side, part.side)].astype(jnp.float32)
            return (
                mine
                + p.landing[4 + half, r, :].astype(jnp.float32)
                + p.landing[3 - half, r, :].astype(jnp.float32)
            )

        @pl.loop(0, part.share // 16)
        def _(i):
            q = pl.ds(pl.multiple_of(i * 16, 16), 16)
            for half in range(2):
                p.pair_out[q, pl.ds(half * part.side, part.side)] = total(
                    half, (1 - zh) * part.share, i, 0
                ).astype(jnp.bfloat16)

        pair_copy(p).start()

        @pl.loop(0, part.share // 16)
        def _(i):
            q = pl.ds(pl.multiple_of(i * 16, 16), 16)
            for half in range(2):
                p.own[q, pl.ds(half * part.side, part.side)] = total(half, zh * part.share, i, 0)

    def hop_first(p, part, weight, mean, square):
        pair_copy(p).wait_recv()

        def piece(i):
            at = part.where(i)
            gradient = p.own[at] + p.pair_in[at].astype(jnp.float32)
            after = adam_apply(weight[at], mean[at], square[at], gradient)
            for k in range(3):
                p.stage[i, k] = after[k]

        @pl.loop(1, n_expert)
        def _(j):
            d = peer(j)
            piece(d)
            remote(
                p.stage.at[d], p.hop_one.at[me], p.one_send.at[d], p.one_recv.at[me], (dp, d)
            ).start()

        piece(me)
        p.hop_one[me] = p.stage[me]

    def hop_second(p, part):
        all_recv(p.stage, p.hop_one, p.one_send, p.one_recv)

        @pl.loop(1, n_expert)
        def _(j):
            d = peer(j)
            p.ordered[d] = p.hop_one[source_of[d]]
            remote(
                p.ordered.at[d], p.hop_two.at[me], p.two_send.at[d], p.two_recv.at[me], (dp, d)
            ).start()

        p.hop_two[me] = p.hop_one[source_of[me]]

    def arrive(p, part, results):
        all_recv(p.ordered, p.hop_two, p.two_send, p.two_recv)

        @pl.loop(0, n_expert)
        def _(i):
            at = part.where(i)
            for k in range(3):
                results[k][at] = p.hop_two[i, k]

    def mix():
        all_recv(produced, returned, back_send, back_recv)
        tok_rows = slot.shape[0]
        width = produced.shape[2]
        cap = produced.shape[1]
        back = returned[...].reshape(n_expert * cap, width)
        lanes = lax.broadcasted_iota(jnp.int32, (tok_rows, n_expert * cap), 1)
        total = None
        for k in range(2):
            pick = (slot[:, k : k + 1] == lanes).astype(jnp.float32).astype(jnp.bfloat16)
            term = gates[:, k : k + 1] * jnp.dot(pick, back, preferred_element_type=jnp.float32)
            total = term if total is None else total + term
        mixed[...] = total.astype(jnp.bfloat16)

    part_in, part_out = parts
    ring_first(pout, part_out, hid_t, upstream)
    all_send(produced, returned, back_send, back_recv)
    ring_first(pin, part_in, tok_t, slope)
    ring_second(pout, part_out)
    ring_second(pin, part_in)
    ring_third(pout, part_out)
    ring_third(pin, part_in)
    mix()
    hop_first(pout, part_out, w_out, m_out, s_out)
    hop_first(pin, part_in, w_in, m_in, s_in)
    hop_second(pout, part_out)
    hop_second(pin, part_in)
    arrive(pout, part_out, outs[4:7])
    arrive(pin, part_in, outs[1:4])
    all_sent(produced, returned, back_send, back_recv)
    for p, part in ((pout, part_out), (pin, part_in)):
        for k in range(6):
            ring_copies(p, part)(k).wait_send()
        pair_copy(p).wait_send()
        all_sent(p.stage, p.hop_one, p.one_send, p.one_recv)
        all_sent(p.ordered, p.hop_two, p.two_send, p.two_recv)


def body(
    tokens,
    route_ids,
    route_gates,
    cotangent,
    old_owner,
    new_owner,
    weight_in,
    weight_out,
    mean_in,
    square_in,
    mean_out,
    square_out,
):
    n_expert = lax.axis_size("expert")
    n_groups = lax.axis_size("dp")
    group = lax.axis_index("dp")
    tok_rows, width = tokens.shape
    picks_each = route_ids.shape[1]
    hidden_width = weight_in.shape[2]
    capacity = 2 * tok_rows * picks_each // n_expert
    slots_all = n_expert * capacity
    rows_in = width // n_groups
    rows_out = hidden_width // n_groups
    experts_all = jnp.arange(n_expert, dtype=jnp.int32)
    picked = (route_ids[:, :, None] == experts_all[None, None, :]).astype(jnp.int32)
    counts = jnp.sum(picked, axis=1)
    before = jnp.cumsum(counts, axis=0) - counts
    position = jnp.sum(picked * before[:, None, :], axis=2)
    slot = jnp.sum(picked * old_owner, axis=2) * capacity + position
    holder = (new_owner[:, None] == experts_all[None, :]).astype(jnp.int32)
    source_of = jnp.sum(holder * old_owner[:, None], axis=0)
    slot_ids = jnp.arange(slots_all, dtype=jnp.int32)
    place = [
        (slot[:, k][None, :] == slot_ids[:, None]).astype(jnp.bfloat16) for k in range(picks_each)
    ]

    def swap(rows):
        return lax.all_to_all(rows, "expert", split_axis=0, concat_axis=0, tiled=True)

    def exchange(rows):
        return swap(rows.reshape(n_expert, capacity, width)).reshape(slots_all, width)

    sent = jnp.dot(sum(place), tokens, preferred_element_type=jnp.float32).astype(jnp.bfloat16)
    arrived = exchange(sent)
    scaled = [
        (route_gates[:, k, None] * cotangent.astype(jnp.float32)).astype(jnp.bfloat16)
        for k in range(picks_each)
    ]
    graded = jnp.dot(
        jnp.concatenate(place, axis=1),
        jnp.concatenate(scaled, axis=0),
        preferred_element_type=jnp.float32,
    ).astype(jnp.bfloat16)
    upstream = exchange(graded)
    preact = jnp.dot(arrived, weight_in[0], preferred_element_type=jnp.float32)
    hidden = jax.nn.silu(preact).astype(jnp.bfloat16)
    produced = jnp.dot(hidden, weight_out[0], preferred_element_type=jnp.float32).astype(
        jnp.bfloat16
    )
    downward = right_dot(upstream, weight_out[0])
    slope = (downward * silu_slope(preact)).astype(jnp.bfloat16)
    in_share = lax.dynamic_slice_in_dim(weight_in[0], group * rows_in, rows_in, 0)
    out_share = lax.dynamic_slice_in_dim(weight_out[0], group * rows_out, rows_out, 0)

    parts = (
        Part(width, hidden_width, (16, hidden_width // 2)),
        Part(hidden_width, width, (rows_out // 2, 128)),
    )
    vmem = pl.BlockSpec(memory_space=pltpu.VMEM)
    smem = pl.BlockSpec(memory_space=pltpu.SMEM)
    shares_in = jax.ShapeDtypeStruct((rows_in, hidden_width), jnp.bfloat16)
    shares_out = jax.ShapeDtypeStruct((rows_out, width), jnp.bfloat16)
    results = pl.pallas_call(
        functools.partial(finish_kernel, n_expert, parts),
        out_shape=[jax.ShapeDtypeStruct((tok_rows, width), jnp.bfloat16)]
        + [shares_in] * 3
        + [shares_out] * 3,
        in_specs=[smem] + [vmem] * 13,
        out_specs=[vmem] * 7,
        scratch_shapes=[
            pltpu.VMEM((n_expert, capacity, width), jnp.bfloat16),
            pltpu.SemaphoreType.DMA((n_expert,)),
            pltpu.SemaphoreType.DMA((n_expert,)),
        ]
        + list(parts[0].scratch(n_expert).values())
        + list(parts[1].scratch(n_expert).values()),
        compiler_params=pltpu.CompilerParams(
            collective_id=0, has_side_effects=True, vmem_limit_bytes=60 << 20
        ),
        name="finish",
    )(
        source_of,
        slot,
        route_gates,
        produced.reshape(n_expert, capacity, width),
        arrived.T,
        slope,
        hidden.T,
        upstream,
        in_share,
        mean_in[0],
        square_in[0],
        out_share,
        mean_out[0],
        square_out[0],
    )
    return (results[0],) + tuple(piece[None] for piece in results[1:])


def solution(mesh):
    return jax.shard_map(
        body,
        mesh=mesh,
        in_specs=(
            P(("dp", "expert"), None),
            P(("dp", "expert"), None),
            P(("dp", "expert"), None),
            P(("dp", "expert"), None),
            P(),
            P(),
            P("expert", None, None),
            P("expert", None, None),
            P("expert", "dp", None),
            P("expert", "dp", None),
            P("expert", "dp", None),
            P("expert", "dp", None),
        ),
        out_specs=(
            P(("dp", "expert"), None),
            P("expert", "dp", None),
            P("expert", "dp", None),
            P("expert", "dp", None),
            P("expert", "dp", None),
            P("expert", "dp", None),
            P("expert", "dp", None),
        ),
        check_vma=False,
    )
```

```python
import functools

import jax
import jax.numpy as jnp
from jax import lax
from jax.experimental import pallas as pl
from jax.experimental.pallas import tpu as pltpu
from jax.sharding import PartitionSpec as P

beta_one = 0.9
beta_two = 0.95
adam_eps = 1e-08
learn_rate = 0.01
adam_step = 100.0
n_ring = 4
n_half = 2
MESH = pl.DeviceIdType.MESH


def silu_slope(preact):
    logistic = jax.nn.sigmoid(preact)
    return logistic * (1.0 + preact * (1.0 - logistic))


def adam_apply(weight, mean_old, square_old, gradient):
    mean_new = beta_one * mean_old.astype(jnp.float32) + (1.0 - beta_one) * gradient
    square_new = beta_two * square_old.astype(jnp.float32) + (1.0 - beta_two) * gradient * gradient
    stride = (
        mean_new
        / (1.0 - beta_one**adam_step)
        / (jnp.sqrt(square_new / (1.0 - beta_two**adam_step)) + adam_eps)
    )
    fresh = (weight.astype(jnp.float32) - learn_rate * stride).astype(jnp.bfloat16)
    return (fresh, mean_new.astype(jnp.bfloat16), square_new.astype(jnp.bfloat16))


def outer_dot(left, right):
    return lax.dot_general(
        left, right, (((0,), (0,)), ((), ())), preferred_element_type=jnp.float32
    )


def right_dot(left, right):
    return lax.dot_general(
        left, right, (((1,), (1,)), ((), ())), preferred_element_type=jnp.float32
    )


def remote(src, dst, send, recv, device):
    return pltpu.make_async_remote_copy(
        src_ref=src, dst_ref=dst, send_sem=send, recv_sem=recv, device_id=device, device_id_type=MESH
    )


class Part:
    def __init__(self, rows, cols, piece):
        self.rows, self.cols, self.piece = rows, cols, piece
        self.share = rows // (n_ring * n_half)
        self.block = rows // n_ring
        self.side = cols // 2
        self.per_row = cols // piece[1]

    def where(self, i):
        r = pl.multiple_of((i // self.per_row) * self.piece[0], 16)
        c = pl.multiple_of((i % self.per_row) * self.piece[1], 128)
        return pl.ds(r, self.piece[0]), pl.ds(c, self.piece[1])

    def scratch(self, n_expert):
        half = (self.block, self.side)
        return dict(
            partial=pltpu.VMEM((self.rows, self.cols), jnp.bfloat16),
            landing=pltpu.VMEM((6,) + half, jnp.bfloat16),
            relayed=pltpu.VMEM((2,) + half, jnp.bfloat16),
            own=pltpu.VMEM((self.share, self.cols), jnp.float32),
            pair_out=pltpu.VMEM((self.share, self.cols), jnp.bfloat16),
            pair_in=pltpu.VMEM((self.share, self.cols), jnp.bfloat16),
            stage=pltpu.VMEM((n_expert, 3) + self.piece, jnp.bfloat16),
            hop_one=pltpu.VMEM((n_expert, 3) + self.piece, jnp.bfloat16),
            hop_two=pltpu.VMEM((n_expert, 3) + self.piece, jnp.bfloat16),
            weight=pltpu.VMEM((self.rows, self.cols), jnp.bfloat16),
            mean=pltpu.VMEM((self.share, self.cols), jnp.bfloat16),
            square=pltpu.VMEM((self.share, self.cols), jnp.bfloat16),
            load=pltpu.SemaphoreType.DMA((3,)),
            ring_send=pltpu.SemaphoreType.DMA((6,)),
            ring_recv=pltpu.SemaphoreType.DMA((6,)),
            pair_send=pltpu.SemaphoreType.DMA,
            pair_recv=pltpu.SemaphoreType.DMA,
            one_send=pltpu.SemaphoreType.DMA((n_expert,)),
            one_recv=pltpu.SemaphoreType.DMA((n_expert,)),
            two_send=pltpu.SemaphoreType.DMA((n_expert,)),
            two_recv=pltpu.SemaphoreType.DMA((n_expert,)),
        )


part_names = tuple(Part(128, 256, (16, 128)).scratch(32))
n_line = 4
n_plane = 8


def flow_scratch(rows, cap, width):
    return dict(
        raw=pltpu.VMEM((n_line, rows, width), jnp.bfloat16),
        sent=pltpu.VMEM((n_line, n_plane, cap, width), jnp.bfloat16),
        came=pltpu.VMEM((n_line, n_plane, cap, width), jnp.bfloat16),
        load=pltpu.SemaphoreType.DMA,
        z_send=pltpu.SemaphoreType.DMA((2, n_line)),
        z_recv=pltpu.SemaphoreType.DMA((n_line,)),
        y_send=pltpu.SemaphoreType.DMA((n_line, n_plane)),
        y_recv=pltpu.SemaphoreType.DMA((n_line, n_plane)),
    )


flow_names = tuple(flow_scratch(128, 16, 2048))


def other_scratch(rows, cap, width, hidden, n_expert):
    slots = n_expert * cap
    return dict(
        meta=pltpu.VMEM((n_line, 8, rows), jnp.float32),
        meta_send=pltpu.SemaphoreType.DMA((2, n_line)),
        meta_recv=pltpu.SemaphoreType.DMA((n_line,)),
        table=pltpu.VMEM((rows, 128), jnp.float32),
        preact=pltpu.VMEM((slots, hidden), jnp.float32),
        hid_t=pltpu.VMEM((hidden, slots), jnp.bfloat16),
        tok_t=pltpu.VMEM((width, slots), jnp.bfloat16),
        slope=pltpu.VMEM((slots, hidden), jnp.bfloat16),
        returned=pltpu.VMEM((n_expert, cap, width), jnp.bfloat16),
        back_send=pltpu.SemaphoreType.DMA((n_expert,)),
        back_recv=pltpu.SemaphoreType.DMA((n_expert,)),
    )


other_names = tuple(other_scratch(128, 16, 2048, 768, 32))


class Refs:
    def __init__(self, names, refs):
        for name, ref in zip(names, refs):
            setattr(self, name, ref)


def whole_kernel(n_expert, parts, *refs):
    (
        source_of,
        owner,
        route_ids,
        gates,
        tokens,
        cotangent,
        w_in,
        m_in,
        s_in,
        w_out,
        m_out,
        s_out,
    ) = refs[:12]
    outs = refs[12:19]
    mixed = outs[0]
    rest = list(refs[19:])

    def take(names):
        group = Refs(names, rest[: len(names)])
        del rest[: len(names)]
        return group

    tok, cot = take(flow_names), take(flow_names)
    sc = take(other_names)
    pin, pout = take(part_names), take(part_names)
    part_in, part_out = parts
    rows, width = mixed.shape
    cap = sc.returned.shape[1]
    slots = n_expert * cap
    dp = lax.axis_index("dp")
    me = lax.axis_index("expert")
    x, zh = dp // 2, dp % 2
    ahead, behind, across = (x + 1) % 4, (x + 3) % 4, (x + 2) % 4
    to_ahead = (ahead * 2 + zh, me)
    to_behind = (behind * 2 + zh, me)
    to_pair = (x * 2 + 1 - zh, me)
    peers = n_expert - 1
    zl = (me // 2) % n_line
    mine = (me // 8) * 2 + me % 2

    def peer(j):
        return (me + j) % n_expert

    def loads():
        plan = [
            (tokens, tok.raw.at[zl], tok.load),
            (cotangent, cot.raw.at[zl], cot.load),
        ]
        for p, sources in ((pin, (w_in, m_in, s_in)), (pout, (w_out, m_out, s_out))):
            for k, target in enumerate((p.weight, p.mean, p.square)):
                plan.append((sources[k], target, p.load.at[k]))
        return plan

    def load(k):
        return pltpu.make_async_copy(*loads()[k])

    for k in range(8):
        load(k).start()

    barrier = pltpu.get_barrier_semaphore()

    @pl.loop(1, n_expert)
    def _(j):
        pl.semaphore_signal(barrier, inc=1, device_id=(dp, peer(j)), device_id_type=MESH)

    for device in (to_ahead, to_behind, to_pair):
        pl.semaphore_signal(barrier, inc=1, device_id=device, device_id_type=MESH)

    def place_own():
        lanes = lax.broadcasted_iota(jnp.int32, (rows, n_expert), 1)
        picked = [(route_ids[:, k : k + 1] == lanes).astype(jnp.float32) for k in range(2)]
        earlier = (
            lax.broadcasted_iota(jnp.int32, (rows, rows), 1)
            < lax.broadcasted_iota(jnp.int32, (rows, rows), 0)
        ).astype(jnp.float32)
        before = jnp.dot(
            earlier.astype(jnp.bfloat16),
            (picked[0] + picked[1]).astype(jnp.bfloat16),
            preferred_element_type=jnp.float32,
        )
        held = owner[...].astype(jnp.float32) * float(cap)
        slot = [jnp.sum(one * (before + held), axis=1, keepdims=True) for one in picked]
        lane = lax.broadcasted_iota(jnp.int32, (rows, 128), 1)
        table = jnp.where(
            lane == 0,
            slot[0],
            jnp.where(lane == 1, slot[1], jnp.where(lane == 2, gates[:, 0:1], gates[:, 1:2])),
        )
        sc.table[...] = table
        sc.meta[zl] = table.T[0:8, :]

    place_own()
    pl.semaphore_wait(barrier, peers + 3)

    def z_copies(buf, send, recv, direction, block):
        neighbour = (dp, me + 2 if direction == 0 else me - 2)
        return remote(
            buf.at[block], buf.at[block], send.at[direction, block], recv.at[block], neighbour
        )

    def z_send(flow, direction, block):
        z_copies(flow.raw, flow.z_send, flow.z_recv, direction, block).start()
        if flow is tok:
            z_copies(sc.meta, sc.meta_send, sc.meta_recv, direction, block).start()

    def z_wait(flow, direction, block, sent):
        copy = z_copies(flow.raw, flow.z_send, flow.z_recv, direction, block)
        copy.wait_send() if sent else copy.wait_recv()
        if flow is tok:
            copy = z_copies(sc.meta, sc.meta_send, sc.meta_recv, direction, block)
            copy.wait_send() if sent else copy.wait_recv()

    def z_first(flow):
        pl.when(zl < n_line - 1)(lambda: z_send(flow, 0, zl))
        pl.when(zl > 0)(lambda: z_send(flow, 1, zl))

    def z_step(flow, step):
        left, right = zl - 1 - step, zl + 1 + step

        @pl.when(left >= 0)
        def _():
            z_wait(flow, 0, left, False)
            pl.when(zl < n_line - 1)(lambda: z_send(flow, 0, left))

        @pl.when(right < n_line)
        def _():
            z_wait(flow, 1, right, False)
            pl.when(zl > 0)(lambda: z_send(flow, 1, right))

    def z_sent(flow):
        @pl.loop(0, n_line)
        def _(block):
            pl.when((zl < n_line - 1) & (block <= zl))(lambda: z_wait(flow, 0, block, True))
            pl.when((zl > 0) & (block >= zl))(lambda: z_wait(flow, 1, block, True))

    def y_copy(flow, block, q):
        device = (dp, (q // 2) * 8 + zl * 2 + q % 2)
        return remote(
            flow.sent.at[block, q],
            flow.came.at[block, mine],
            flow.y_send.at[block, q],
            flow.y_recv.at[block, mine],
            device,
        )

    def y_got(flow, block, q):
        device = (dp, (q // 2) * 8 + zl * 2 + q % 2)
        return remote(
            flow.sent.at[block, q],
            flow.came.at[block, q],
            flow.y_send.at[block, q],
            flow.y_recv.at[block, q],
            device,
        )

    def y_send(flow, block):
        r = lax.broadcasted_iota(jnp.int32, (n_plane * cap, rows), 0)
        here = ((r // (2 * cap)) * (n_expert * cap // 4) + r % (2 * cap) + zl * (2 * cap)).astype(
            jnp.float32
        )
        pick = [
            (sc.meta[block, k : k + 1, :] == here).astype(jnp.float32).astype(jnp.bfloat16)
            for k in range(2)
        ]
        if flow is tok:
            put = jnp.dot(pick[0] + pick[1], flow.raw[block], preferred_element_type=jnp.float32)
        else:
            put = None
            for k in range(2):
                gate = jnp.broadcast_to(sc.meta[block, 2 + k : 3 + k, :], (rows, rows)).T[:, 0:1]
                scaled = (gate * flow.raw[block].astype(jnp.float32)).astype(jnp.bfloat16)
                term = jnp.dot(pick[k], scaled, preferred_element_type=jnp.float32)
                put = term if put is None else put + term
        flow.sent[block] = put.astype(jnp.bfloat16).reshape(n_plane, cap, width)

        @pl.loop(1, n_plane)
        def _(j):
            y_copy(flow, block, (mine + j) % n_plane).start()

        flow.came[block, mine] = flow.sent[block, mine]

    def y_step(flow, step):
        left, right = zl - 1 - step, zl + 1 + step
        pl.when(left >= 0)(lambda: y_send(flow, left))
        pl.when(right < n_line)(lambda: y_send(flow, right))

    def y_all(flow, sent):
        @pl.loop(0, n_line)
        def _(block):
            @pl.loop(1, n_plane)
            def _(j):
                q = (mine + j) % n_plane
                if sent:
                    y_copy(flow, block, q).wait_send()
                else:
                    y_got(flow, block, q).wait_recv()

    def forward():
        y_all(tok, False)
        y_all(tok, True)
        step = n_plane * cap

        @pl.loop(0, n_line)
        def _(i):
            r = pl.ds(pl.multiple_of(i * step, step), step)
            preact = jnp.dot(
                tok.came[i].reshape(step, width), pin.weight[...], preferred_element_type=jnp.float32
            )
            sc.preact[r, :] = preact
            hidden = jax.nn.silu(preact).astype(jnp.bfloat16)
            tok.sent[i] = (
                jnp.dot(hidden, pout.weight[...], preferred_element_type=jnp.float32)
                .astype(jnp.bfloat16)
                .reshape(n_plane, cap, width)
            )
            sc.hid_t[:, r] = hidden.T

    def turn():
        step = n_plane * cap

        @pl.loop(0, n_line)
        def _(i):
            r = pl.ds(pl.multiple_of(i * step, step), step)
            sc.tok_t[:, r] = tok.came[i].reshape(step, width).T

    def backward():
        step = n_plane * cap

        @pl.loop(0, n_line)
        def _(i):
            r = pl.ds(pl.multiple_of(i * step, step), step)
            downward = right_dot(cot.came[i].reshape(step, width), pout.weight[...])
            sc.slope[r, :] = (downward * silu_slope(sc.preact[r, :])).astype(jnp.bfloat16)

    def back_copy(d, landing):
        block, q = (d // 2) % n_line, (d // 8) * 2 + d % 2
        return remote(
            tok.sent.at[block, q],
            sc.returned.at[landing],
            sc.back_send.at[d],
            sc.back_recv.at[landing],
            (dp, d),
        )

    def back_all(what):
        @pl.loop(1, n_expert)
        def _(j):
            d = peer(j)
            if what == "start":
                back_copy(d, me).start()
            elif what == "recv":
                back_copy(d, d).wait_recv()
            else:
                back_copy(d, me).wait_send()

    def all_wait(src, dst, send, recv, sent):
        @pl.loop(1, n_expert)
        def _(j):
            d = peer(j)
            copy = remote(src.at[d], dst.at[d], send.at[d], recv.at[d], (dp, d))
            copy.wait_send() if sent else copy.wait_recv()

    def ring_copies(p, part):
        def side(block, half):
            r = pl.multiple_of(block * part.block, 16)
            return p.partial.at[pl.ds(r, part.block), pl.ds(half * part.side, part.side)]

        plan = [
            (side(across, 0), 0, to_ahead),
            (side(across, 1), 1, to_behind),
            (side(ahead, 1), 2, to_ahead),
            (side(behind, 0), 3, to_behind),
            (p.relayed.at[0], 4, to_ahead),
            (p.relayed.at[1], 5, to_behind),
        ]
        def copy(k):
            src, slot_of, device = plan[k]
            return remote(
                src, p.landing.at[slot_of], p.ring_send.at[k], p.ring_recv.at[k], device
            )

        return copy

    def ring_first(p, part, left, right):
        def fill(block):
            step = min(part.block, 256)
            base = block * part.block

            @pl.loop(0, part.block // step)
            def _(i):
                r = pl.ds(pl.multiple_of(base + i * step, 16), step)
                p.partial[r, :] = jnp.dot(
                    left[r, :], right(), preferred_element_type=jnp.float32
                ).astype(jnp.bfloat16)

        copies = ring_copies(p, part)
        fill(across)
        copies(0).start()
        copies(1).start()
        fill(ahead)
        copies(2).start()
        fill(behind)
        copies(3).start()
        fill(x)

    def ring_second(p, part):
        copies = ring_copies(p, part)
        for k, block in ((0, ahead), (1, behind)):
            copies(k).wait_recv()

            @pl.loop(0, part.block // 16)
            def _(i):
                r = pl.ds(pl.multiple_of(i * 16, 16), 16)
                q = pl.ds(pl.multiple_of(block * part.block + i * 16, 16), 16)
                mine = p.partial[q, pl.ds(k * part.side, part.side)].astype(jnp.float32)
                p.relayed[k, r, :] = (p.landing[k, r, :].astype(jnp.float32) + mine).astype(
                    jnp.bfloat16
                )

            copies(4 + k).start()

    def pair_copy(p):
        return remote(p.pair_out, p.pair_in, p.pair_send, p.pair_recv, to_pair)

    def ring_third(p, part):
        copies = ring_copies(p, part)
        for k in (2, 3, 4, 5):
            copies(k).wait_recv()

        def total(half, base, i, k):
            r = pl.ds(pl.multiple_of(base + i * 16, 16), 16)
            q = pl.ds(pl.multiple_of(x * part.block + base + i * 16, 16), 16)
            mine = p.partial[q, pl.ds(half * part.side, part.side)].astype(jnp.float32)
            return (
                mine
                + p.landing[4 + half, r, :].astype(jnp.float32)
                + p.landing[3 - half, r, :].astype(jnp.float32)
            )

        @pl.loop(0, part.share // 16)
        def _(i):
            q = pl.ds(pl.multiple_of(i * 16, 16), 16)
            for half in range(2):
                p.pair_out[q, pl.ds(half * part.side, part.side)] = total(
                    half, (1 - zh) * part.share, i, 0
                ).astype(jnp.bfloat16)

        pair_copy(p).start()

        @pl.loop(0, part.share // 16)
        def _(i):
            q = pl.ds(pl.multiple_of(i * 16, 16), 16)
            for half in range(2):
                p.own[q, pl.ds(half * part.side, part.side)] = total(half, zh * part.share, i, 0)

    def hop_first(p, part):
        pair_copy(p).wait_recv()

        def piece(i):
            at = part.where(i)
            r = (i // part.per_row) * part.piece[0] + dp * part.share
            weight = p.weight[pl.ds(pl.multiple_of(r, 16), part.piece[0]), at[1]]
            gradient = p.own[at] + p.pair_in[at].astype(jnp.float32)
            after = adam_apply(weight, p.mean[at], p.square[at], gradient)
            for k in range(3):
                p.stage[i, k] = after[k]

        @pl.loop(1, n_expert)
        def _(j):
            d = peer(j)
            piece(d)
            remote(
                p.stage.at[d], p.hop_one.at[me], p.one_send.at[d], p.one_recv.at[me], (dp, d)
            ).start()

        piece(me)
        p.hop_one[me] = p.stage[me]

    def hop_second(p, part):
        all_wait(p.stage, p.hop_one, p.one_send, p.one_recv, True)
        all_wait(p.stage, p.hop_one, p.one_send, p.one_recv, False)

        @pl.loop(1, n_expert)
        def _(j):
            d = peer(j)
            p.stage[d] = p.hop_one[source_of[d]]
            remote(
                p.stage.at[d], p.hop_two.at[me], p.two_send.at[d], p.two_recv.at[me], (dp, d)
            ).start()

        p.hop_two[me] = p.hop_one[source_of[me]]

    def arrive(p, part, results):
        all_wait(p.stage, p.hop_two, p.two_send, p.two_recv, False)

        @pl.loop(0, n_expert)
        def _(i):
            at = part.where(i)
            for k in range(3):
                results[k][at] = p.hop_two[i, k]

    def mix():
        back_all("recv")
        back = sc.returned[...].reshape(slots, width)
        lanes = lax.broadcasted_iota(jnp.int32, (rows, slots), 1).astype(jnp.float32)
        total = None
        for k in range(2):
            pick = (sc.table[:, k : k + 1] == lanes).astype(jnp.float32).astype(jnp.bfloat16)
            term = gates[:, k : k + 1] * jnp.dot(pick, back, preferred_element_type=jnp.float32)
            total = term if total is None else total + term
        mixed[...] = total.astype(jnp.bfloat16)

    load(0).wait()
    z_first(tok)
    y_send(tok, zl)
    load(1).wait()
    z_step(tok, 0)
    z_first(cot)
    y_step(tok, 0)

    @pl.loop(1, n_line - 1)
    def _(step):
        z_step(tok, step)
        y_step(tok, step)

    y_send(cot, zl)
    z_step(cot, 0)
    y_step(cot, 0)
    for k in range(2, 8):
        load(k).wait()
    forward()

    @pl.loop(1, n_line - 1)
    def _(step):
        z_step(cot, step)
        y_step(cot, step)

    turn()
    y_all(cot, False)
    ring_first(pout, part_out, sc.hid_t, lambda: cot.came[...].reshape(slots, width))
    back_all("start")
    sc.returned[me] = tok.sent[zl, mine]
    backward()
    ring_first(pin, part_in, sc.tok_t, lambda: sc.slope[...])
    ring_second(pout, part_out)
    ring_second(pin, part_in)
    ring_third(pout, part_out)
    ring_third(pin, part_in)
    mix()
    hop_first(pout, part_out)
    hop_first(pin, part_in)
    hop_second(pout, part_out)
    hop_second(pin, part_in)
    arrive(pout, part_out, outs[4:7])
    arrive(pin, part_in, outs[1:4])
    z_sent(tok)
    z_sent(cot)
    y_all(cot, True)
    back_all("sent")
    for p, part in ((pout, part_out), (pin, part_in)):
        for k in range(6):
            ring_copies(p, part)(k).wait_send()
        pair_copy(p).wait_send()
        all_wait(p.stage, p.hop_two, p.two_send, p.two_recv, True)


def body(
    tokens,
    route_ids,
    route_gates,
    cotangent,
    old_owner,
    new_owner,
    weight_in,
    weight_out,
    mean_in,
    square_in,
    mean_out,
    square_out,
):
    n_expert = lax.axis_size("expert")
    n_groups = lax.axis_size("dp")
    tok_rows, width = tokens.shape
    picks_each = route_ids.shape[1]
    hidden_width = weight_in.shape[2]
    capacity = 2 * tok_rows * picks_each // n_expert
    rows_in = width // n_groups
    rows_out = hidden_width // n_groups
    experts_all = jnp.arange(n_expert, dtype=jnp.int32)
    holder = (new_owner[:, None] == experts_all[None, :]).astype(jnp.int32)
    source_of = jnp.sum(holder * old_owner[:, None], axis=0)
    parts = (
        Part(width, hidden_width, (16, hidden_width // 2)),
        Part(hidden_width, width, (rows_out // 2, 128)),
    )
    vmem = pl.BlockSpec(memory_space=pltpu.VMEM)
    smem = pl.BlockSpec(memory_space=pltpu.SMEM)
    far = pl.BlockSpec(memory_space=pl.ANY)
    shares_in = jax.ShapeDtypeStruct((rows_in, hidden_width), jnp.bfloat16)
    shares_out = jax.ShapeDtypeStruct((rows_out, width), jnp.bfloat16)
    flow = list(flow_scratch(tok_rows, capacity, width).values())
    other = other_scratch(tok_rows, capacity, width, hidden_width, n_expert)
    results = pl.pallas_call(
        functools.partial(whole_kernel, n_expert, parts),
        out_shape=[jax.ShapeDtypeStruct((tok_rows, width), jnp.bfloat16)]
        + [shares_in] * 3
        + [shares_out] * 3,
        in_specs=[smem] + [vmem] * 3 + [far] * 8,
        out_specs=[vmem] * 7,
        scratch_shapes=flow
        + flow
        + list(other.values())
        + list(parts[0].scratch(n_expert).values())
        + list(parts[1].scratch(n_expert).values()),
        compiler_params=pltpu.CompilerParams(
            collective_id=0, has_side_effects=True, vmem_limit_bytes=63 << 20
        ),
        name="whole",
    )(
        source_of,
        old_owner.reshape(1, n_expert),
        route_ids,
        route_gates,
        tokens,
        cotangent,
        weight_in[0],
        mean_in[0],
        square_in[0],
        weight_out[0],
        mean_out[0],
        square_out[0],
    )
    return (results[0],) + tuple(piece[None] for piece in results[1:])


def solution(mesh):
    return jax.shard_map(
        body,
        mesh=mesh,
        in_specs=(
            P(("dp", "expert"), None),
            P(("dp", "expert"), None),
            P(("dp", "expert"), None),
            P(("dp", "expert"), None),
            P(),
            P(),
            P("expert", None, None),
            P("expert", None, None),
            P("expert", "dp", None),
            P("expert", "dp", None),
            P("expert", "dp", None),
            P("expert", "dp", None),
        ),
        out_specs=(
            P(("dp", "expert"), None),
            P("expert", "dp", None),
            P("expert", "dp", None),
            P("expert", "dp", None),
            P("expert", "dp", None),
            P("expert", "dp", None),
            P("expert", "dp", None),
        ),
        check_vma=False,
    )
```

```python
import functools

import jax
import jax.numpy as jnp
from jax import lax
from jax.experimental import pallas as pl
from jax.experimental.pallas import tpu as pltpu
from jax.sharding import PartitionSpec as P

beta_one = 0.9
beta_two = 0.95
adam_eps = 1e-08
learn_rate = 0.01
adam_step = 100.0
n_ring = 4
n_half = 2
MESH = pl.DeviceIdType.MESH


def silu_slope(preact):
    logistic = jax.nn.sigmoid(preact)
    return logistic * (1.0 + preact * (1.0 - logistic))


def adam_moments(mean_old, square_old, gradient):
    mean_new = beta_one * mean_old.astype(jnp.float32) + (1.0 - beta_one) * gradient
    square_new = beta_two * square_old.astype(jnp.float32) + (1.0 - beta_two) * gradient * gradient
    return mean_new.astype(jnp.bfloat16), square_new.astype(jnp.bfloat16)


def adam_weight(weight, mean_new, square_new):
    stride = (
        mean_new.astype(jnp.float32)
        / (1.0 - beta_one**adam_step)
        / (jnp.sqrt(square_new.astype(jnp.float32) / (1.0 - beta_two**adam_step)) + adam_eps)
    )
    return (weight.astype(jnp.float32) - learn_rate * stride).astype(jnp.bfloat16)


def outer_dot(left, right):
    return lax.dot_general(
        left, right, (((0,), (0,)), ((), ())), preferred_element_type=jnp.float32
    )


def right_dot(left, right):
    return lax.dot_general(
        left, right, (((1,), (1,)), ((), ())), preferred_element_type=jnp.float32
    )


def remote(src, dst, send, recv, device):
    return pltpu.make_async_remote_copy(
        src_ref=src, dst_ref=dst, send_sem=send, recv_sem=recv, device_id=device, device_id_type=MESH
    )


class Part:
    def __init__(self, rows, cols, piece):
        self.rows, self.cols, self.piece = rows, cols, piece
        self.share = rows // (n_ring * n_half)
        self.block = rows // n_ring
        self.side = cols // 2
        self.per_row = cols // piece[1]

    def where(self, i):
        r = pl.multiple_of((i // self.per_row) * self.piece[0], 16)
        c = pl.multiple_of((i % self.per_row) * self.piece[1], 128)
        return pl.ds(r, self.piece[0]), pl.ds(c, self.piece[1])

    def scratch(self, n_expert):
        half = (self.block, self.side)
        return dict(
            partial=pltpu.VMEM((self.rows, self.cols), jnp.bfloat16),
            landing=pltpu.VMEM((6,) + half, jnp.bfloat16),
            relayed=pltpu.VMEM((2,) + half, jnp.bfloat16),
            own=pltpu.VMEM((self.share, self.cols), jnp.float32),
            pair_out=pltpu.VMEM((self.share, self.cols), jnp.bfloat16),
            pair_in=pltpu.VMEM((self.share, self.cols), jnp.bfloat16),
            stage=pltpu.VMEM((n_expert, 2) + self.piece, jnp.bfloat16),
            hop_one=pltpu.VMEM((n_expert, 2) + self.piece, jnp.bfloat16),
            hop_two=pltpu.VMEM((n_expert, 2) + self.piece, jnp.bfloat16),
            w_one=pltpu.VMEM((n_expert,) + self.piece, jnp.bfloat16),
            w_stage=pltpu.VMEM((n_expert,) + self.piece, jnp.bfloat16),
            w_two=pltpu.VMEM((n_expert,) + self.piece, jnp.bfloat16),
            w_one_send=pltpu.SemaphoreType.DMA((n_expert,)),
            w_one_recv=pltpu.SemaphoreType.DMA((n_expert,)),
            w_two_send=pltpu.SemaphoreType.DMA((n_expert,)),
            w_two_recv=pltpu.SemaphoreType.DMA((n_expert,)),
            weight=pltpu.VMEM((self.rows, self.cols), jnp.bfloat16),
            mean=pltpu.VMEM((self.share, self.cols), jnp.bfloat16),
            square=pltpu.VMEM((self.share, self.cols), jnp.bfloat16),
            load=pltpu.SemaphoreType.DMA((3,)),
            ring_send=pltpu.SemaphoreType.DMA((6,)),
            ring_recv=pltpu.SemaphoreType.DMA((6,)),
            pair_send=pltpu.SemaphoreType.DMA,
            pair_recv=pltpu.SemaphoreType.DMA,
            one_send=pltpu.SemaphoreType.DMA((n_expert,)),
            one_recv=pltpu.SemaphoreType.DMA((n_expert,)),
            two_send=pltpu.SemaphoreType.DMA((n_expert,)),
            two_recv=pltpu.SemaphoreType.DMA((n_expert,)),
        )


part_names = tuple(Part(128, 256, (16, 128)).scratch(32))
n_line = 4
n_plane = 8


def flow_scratch(rows, cap, width):
    return dict(
        raw=pltpu.VMEM((n_line, rows, width), jnp.bfloat16),
        sent=pltpu.VMEM((n_line, n_plane, cap, width), jnp.bfloat16),
        came=pltpu.VMEM((n_line, n_plane, cap, width), jnp.bfloat16),
        load=pltpu.SemaphoreType.DMA,
        z_send=pltpu.SemaphoreType.DMA((2, n_line)),
        z_recv=pltpu.SemaphoreType.DMA((n_line,)),
        y_send=pltpu.SemaphoreType.DMA((n_line, n_plane)),
        y_recv=pltpu.SemaphoreType.DMA((n_line, n_plane)),
    )


flow_names = tuple(flow_scratch(128, 16, 2048))


def other_scratch(rows, cap, width, hidden, n_expert):
    slots = n_expert * cap
    return dict(
        meta=pltpu.VMEM((n_line, 8, rows), jnp.float32),
        meta_send=pltpu.SemaphoreType.DMA((2, n_line)),
        meta_recv=pltpu.SemaphoreType.DMA((n_line,)),
        preact=pltpu.VMEM((slots, hidden), jnp.float32),
        hid_t=pltpu.VMEM((hidden, slots), jnp.bfloat16),
        tok_t=pltpu.VMEM((width, slots), jnp.bfloat16),
        slope=pltpu.VMEM((slots, hidden), jnp.bfloat16),
        returned=pltpu.VMEM((n_expert, cap, width), jnp.bfloat16),
        back_send=pltpu.SemaphoreType.DMA((n_expert,)),
        back_recv=pltpu.SemaphoreType.DMA((n_expert,)),
    )


other_names = tuple(other_scratch(128, 16, 2048, 768, 32))


class Refs:
    def __init__(self, names, refs):
        for name, ref in zip(names, refs):
            setattr(self, name, ref)


def whole_kernel(n_expert, parts, *refs):
    (
        source_of,
        owner,
        route_ids,
        gates,
        tokens,
        cotangent,
        w_in,
        m_in,
        s_in,
        w_out,
        m_out,
        s_out,
    ) = refs[:12]
    outs = refs[12:19]
    mixed = outs[0]
    rest = list(refs[19:])

    def take(names):
        group = Refs(names, rest[: len(names)])
        del rest[: len(names)]
        return group

    tok, cot = take(flow_names), take(flow_names)
    sc = take(other_names)
    pin, pout = take(part_names), take(part_names)
    part_in, part_out = parts
    rows, width = mixed.shape
    cap = sc.returned.shape[1]
    slots = n_expert * cap
    dp = lax.axis_index("dp")
    me = lax.axis_index("expert")
    x, zh = dp // 2, dp % 2
    ahead, behind, across = (x + 1) % 4, (x + 3) % 4, (x + 2) % 4
    to_ahead = (ahead * 2 + zh, me)
    to_behind = (behind * 2 + zh, me)
    to_pair = (x * 2 + 1 - zh, me)
    peers = n_expert - 1
    zl = (me // 2) % n_line
    mine = (me // 8) * 2 + me % 2

    def peer(j):
        return (me + j) % n_expert

    def other_half(i):
        apart = (i // 2) % n_line - zl
        return (
            (apart == 3)
            | (apart == -3)
            | (((apart == 2) | (apart == -2)) & (i % 2 == me % 2))
        )

    def loads():
        plan = [
            (tokens, tok.raw.at[zl], tok.load),
            (cotangent, cot.raw.at[zl], cot.load),
        ]
        for p, sources in ((pin, (w_in, m_in, s_in)), (pout, (w_out, m_out, s_out))):
            for k, target in enumerate((p.weight, p.mean, p.square)):
                plan.append((sources[k], target, p.load.at[k]))
        return plan

    def load(k):
        return pltpu.make_async_copy(*loads()[k])

    for k in range(8):
        load(k).start()

    barrier = pltpu.get_barrier_semaphore()

    @pl.loop(1, n_expert)
    def _(j):
        pl.semaphore_signal(barrier, inc=1, device_id=(dp, peer(j)), device_id_type=MESH)

    for device in (to_ahead, to_behind, to_pair):
        pl.semaphore_signal(barrier, inc=1, device_id=device, device_id_type=MESH)

    @pl.loop(0, n_expert)
    def _(i):
        @pl.when(other_half(i))
        def _():
            pl.semaphore_signal(
                barrier, inc=1, device_id=(x * 2 + 1 - zh, i), device_id_type=MESH
            )


    def place_own():
        def column(ref, k):
            return jnp.broadcast_to(ref[k : k + 1, :].astype(jnp.float32), (rows, rows)).T

        lanes = lax.broadcasted_iota(jnp.int32, (rows, n_expert), 1).astype(jnp.float32)
        picked = [(column(route_ids, k)[:, 0:1] == lanes).astype(jnp.float32) for k in range(2)]
        earlier = (
            lax.broadcasted_iota(jnp.int32, (rows, rows), 1)
            < lax.broadcasted_iota(jnp.int32, (rows, rows), 0)
        ).astype(jnp.float32)
        before = jnp.dot(
            earlier.astype(jnp.bfloat16),
            (picked[0] + picked[1]).astype(jnp.bfloat16),
            preferred_element_type=jnp.float32,
        )
        held = owner[...].astype(jnp.float32) * float(cap)
        slot = [jnp.sum(one * (before + held), axis=1, keepdims=True) for one in picked]
        lane = lax.broadcasted_iota(jnp.int32, (rows, 128), 1)
        table = jnp.where(
            lane == 0,
            slot[0],
            jnp.where(lane == 1, slot[1], jnp.where(lane == 2, column(gates, 0), column(gates, 1))),
        )
        sc.meta[zl] = table.T[0:8, :]

    place_own()
    far_half = jnp.where((zl == 0) | (zl == n_line - 1), 12, 4)
    pl.semaphore_wait(barrier, peers + 3 + far_half)

    def z_copies(buf, send, recv, direction, block):
        neighbour = (dp, me + 2 if direction == 0 else me - 2)
        return remote(
            buf.at[block], buf.at[block], send.at[direction, block], recv.at[block], neighbour
        )

    def z_send(flow, direction, block):
        z_copies(flow.raw, flow.z_send, flow.z_recv, direction, block).start()
        if flow is tok:
            z_copies(sc.meta, sc.meta_send, sc.meta_recv, direction, block).start()

    def z_wait(flow, direction, block, sent):
        copy = z_copies(flow.raw, flow.z_send, flow.z_recv, direction, block)
        copy.wait_send() if sent else copy.wait_recv()
        if flow is tok:
            copy = z_copies(sc.meta, sc.meta_send, sc.meta_recv, direction, block)
            copy.wait_send() if sent else copy.wait_recv()

    def z_first(flow):
        pl.when(zl < n_line - 1)(lambda: z_send(flow, 0, zl))
        pl.when(zl > 0)(lambda: z_send(flow, 1, zl))

    def z_step(flow, step):
        left, right = zl - 1 - step, zl + 1 + step

        @pl.when(left >= 0)
        def _():
            z_wait(flow, 0, left, False)
            pl.when(zl < n_line - 1)(lambda: z_send(flow, 0, left))

        @pl.when(right < n_line)
        def _():
            z_wait(flow, 1, right, False)
            pl.when(zl > 0)(lambda: z_send(flow, 1, right))

    def z_sent(flow):
        @pl.loop(0, n_line)
        def _(block):
            pl.when((zl < n_line - 1) & (block <= zl))(lambda: z_wait(flow, 0, block, True))
            pl.when((zl > 0) & (block >= zl))(lambda: z_wait(flow, 1, block, True))

    def y_copy(flow, block, q):
        device = (dp, (q // 2) * 8 + zl * 2 + q % 2)
        return remote(
            flow.sent.at[block, q],
            flow.came.at[block, mine],
            flow.y_send.at[block, q],
            flow.y_recv.at[block, mine],
            device,
        )

    def y_got(flow, block, q):
        device = (dp, (q // 2) * 8 + zl * 2 + q % 2)
        return remote(
            flow.sent.at[block, q],
            flow.came.at[block, q],
            flow.y_send.at[block, q],
            flow.y_recv.at[block, q],
            device,
        )

    def y_send(flow, block):
        r = lax.broadcasted_iota(jnp.int32, (n_plane * cap, rows), 0)
        here = ((r // (2 * cap)) * (n_expert * cap // 4) + r % (2 * cap) + zl * (2 * cap)).astype(
            jnp.float32
        )
        pick = [
            (sc.meta[block, k : k + 1, :] == here).astype(jnp.float32).astype(jnp.bfloat16)
            for k in range(2)
        ]
        if flow is tok:
            put = jnp.dot(pick[0] + pick[1], flow.raw[block], preferred_element_type=jnp.float32)
        else:
            put = None
            for k in range(2):
                gate = jnp.broadcast_to(sc.meta[block, 2 + k : 3 + k, :], (rows, rows)).T[:, 0:1]
                scaled = (gate * flow.raw[block].astype(jnp.float32)).astype(jnp.bfloat16)
                term = jnp.dot(pick[k], scaled, preferred_element_type=jnp.float32)
                put = term if put is None else put + term
        flow.sent[block] = put.astype(jnp.bfloat16).reshape(n_plane, cap, width)

        @pl.loop(1, n_plane)
        def _(j):
            y_copy(flow, block, (mine + j) % n_plane).start()

        flow.came[block, mine] = flow.sent[block, mine]

    def y_step(flow, step):
        left, right = zl - 1 - step, zl + 1 + step
        pl.when(left >= 0)(lambda: y_send(flow, left))
        pl.when(right < n_line)(lambda: y_send(flow, right))

    def y_all(flow, sent):
        @pl.loop(0, n_line)
        def _(block):
            @pl.loop(1, n_plane)
            def _(j):
                q = (mine + j) % n_plane
                if sent:
                    y_copy(flow, block, q).wait_send()
                else:
                    y_got(flow, block, q).wait_recv()

    def forward():
        y_all(tok, False)
        y_all(tok, True)
        step = n_plane * cap

        @pl.loop(0, n_line)
        def _(i):
            r = pl.ds(pl.multiple_of(i * step, step), step)
            preact = jnp.dot(
                tok.came[i].reshape(step, width), pin.weight[...], preferred_element_type=jnp.float32
            )
            sc.preact[r, :] = preact
            hidden = jax.nn.silu(preact).astype(jnp.bfloat16)
            tok.sent[i] = (
                jnp.dot(hidden, pout.weight[...], preferred_element_type=jnp.float32)
                .astype(jnp.bfloat16)
                .reshape(n_plane, cap, width)
            )
            sc.hid_t[:, r] = hidden.T

    def turn():
        step = n_plane * cap

        @pl.loop(0, n_line)
        def _(i):
            r = pl.ds(pl.multiple_of(i * step, step), step)
            sc.tok_t[:, r] = tok.came[i].reshape(step, width).T

    def backward():
        step = n_plane * cap

        @pl.loop(0, n_line)
        def _(i):
            r = pl.ds(pl.multiple_of(i * step, step), step)
            downward = right_dot(cot.came[i].reshape(step, width), pout.weight[...])
            sc.slope[r, :] = (downward * silu_slope(sc.preact[r, :])).astype(jnp.bfloat16)

    def back_copy(d, landing):
        block, q = (d // 2) % n_line, (d // 8) * 2 + d % 2
        return remote(
            tok.sent.at[block, q],
            sc.returned.at[landing],
            sc.back_send.at[d],
            sc.back_recv.at[landing],
            (dp, d),
        )

    def back_all(what):
        @pl.loop(1, n_expert)
        def _(j):
            d = peer(j)
            if what == "start":
                back_copy(d, me).start()
            elif what == "recv":
                back_copy(d, d).wait_recv()
            else:
                back_copy(d, me).wait_send()

        if what == "start":
            sc.returned[me] = tok.sent[zl, mine]

    def mix():
        back_all("recv")
        back = sc.returned[...].reshape(slots, width)
        lanes = lax.broadcasted_iota(jnp.int32, (rows, slots), 1).astype(jnp.float32)
        total = None
        for k in range(2):
            slot = jnp.broadcast_to(sc.meta[zl, k : k + 1, :], (rows, rows)).T[:, 0:1]
            gate = jnp.broadcast_to(sc.meta[zl, 2 + k : 3 + k, :], (rows, rows)).T[:, 0:1]
            pick = (slot == lanes).astype(jnp.float32).astype(jnp.bfloat16)
            term = gate * jnp.dot(pick, back, preferred_element_type=jnp.float32)
            total = term if total is None else total + term
        mixed[...] = total.astype(jnp.bfloat16)

    def all_wait(src, dst, send, recv, sent):
        @pl.loop(1, n_expert)
        def _(j):
            d = peer(j)
            copy = remote(src.at[d], dst.at[d], send.at[d], recv.at[d], (dp, d))
            copy.wait_send() if sent else copy.wait_recv()

    def ring_copies(p, part):
        def side(block, half):
            r = pl.multiple_of(block * part.block, 16)
            return p.partial.at[pl.ds(r, part.block), pl.ds(half * part.side, part.side)]

        plan = [
            (side(across, 0), 0, to_ahead),
            (side(across, 1), 1, to_behind),
            (side(ahead, 1), 2, to_ahead),
            (side(behind, 0), 3, to_behind),
            (p.relayed.at[0], 4, to_ahead),
            (p.relayed.at[1], 5, to_behind),
        ]
        def copy(k):
            src, slot_of, device = plan[k]
            return remote(
                src, p.landing.at[slot_of], p.ring_send.at[k], p.ring_recv.at[k], device
            )

        return copy

    def ring_first(p, part, left, right):
        def fill(block):
            step = min(part.block, 256)
            base = block * part.block

            @pl.loop(0, part.block // step)
            def _(i):
                r = pl.ds(pl.multiple_of(base + i * step, 16), step)
                p.partial[r, :] = jnp.dot(
                    left[r, :], right(), preferred_element_type=jnp.float32
                ).astype(jnp.bfloat16)

        copies = ring_copies(p, part)
        fill(across)
        copies(0).start()
        copies(1).start()
        fill(ahead)
        copies(2).start()
        fill(behind)
        copies(3).start()
        fill(x)

    def ring_second(p, part):
        copies = ring_copies(p, part)
        for k, block in ((0, ahead), (1, behind)):
            copies(k).wait_recv()

            @pl.loop(0, part.block // 16)
            def _(i):
                r = pl.ds(pl.multiple_of(i * 16, 16), 16)
                q = pl.ds(pl.multiple_of(block * part.block + i * 16, 16), 16)
                mine = p.partial[q, pl.ds(k * part.side, part.side)].astype(jnp.float32)
                p.relayed[k, r, :] = (p.landing[k, r, :].astype(jnp.float32) + mine).astype(
                    jnp.bfloat16
                )

            copies(4 + k).start()

    def pair_copy(p):
        return remote(p.pair_out, p.pair_in, p.pair_send, p.pair_recv, to_pair)

    def ring_third(p, part):
        copies = ring_copies(p, part)
        for k in (2, 3, 4, 5):
            copies(k).wait_recv()

        def total(half, base, i, k):
            r = pl.ds(pl.multiple_of(base + i * 16, 16), 16)
            q = pl.ds(pl.multiple_of(x * part.block + base + i * 16, 16), 16)
            mine = p.partial[q, pl.ds(half * part.side, part.side)].astype(jnp.float32)
            return (
                mine
                + p.landing[4 + half, r, :].astype(jnp.float32)
                + p.landing[3 - half, r, :].astype(jnp.float32)
            )

        @pl.loop(0, part.share // 16)
        def _(i):
            q = pl.ds(pl.multiple_of(i * 16, 16), 16)
            for half in range(2):
                p.pair_out[q, pl.ds(half * part.side, part.side)] = total(
                    half, (1 - zh) * part.share, i, 0
                ).astype(jnp.bfloat16)

        pair_copy(p).start()

        @pl.loop(0, part.share // 16)
        def _(i):
            q = pl.ds(pl.multiple_of(i * 16, 16), 16)
            for half in range(2):
                p.own[q, pl.ds(half * part.side, part.side)] = total(half, zh * part.share, i, 0)

    def w_copy(p, part, i):
        to = x * 2 + jnp.where(other_half(i), 1 - zh, zh)
        at = part.where(i)
        r = (i // part.per_row) * part.piece[0] + to * part.share
        source = p.weight.at[pl.ds(pl.multiple_of(r, 16), part.piece[0]), at[1]]
        return remote(source, p.w_one.at[me], p.w_one_send.at[i], p.w_one_recv.at[me], (to, i))

    def w_first(p, part):
        @pl.loop(1, n_expert)
        def _(j):
            w_copy(p, part, peer(j)).start()

        at = part.where(me)
        r = (me // part.per_row) * part.piece[0] + dp * part.share
        p.w_one[me] = p.weight[pl.ds(pl.multiple_of(r, 16), part.piece[0]), at[1]]

    def w_sent(p, part):
        @pl.loop(1, n_expert)
        def _(j):
            w_copy(p, part, peer(j)).wait_send()

    def w_second(p, part):
        all_wait(p.w_stage, p.w_one, p.w_one_send, p.w_one_recv, False)

        @pl.loop(1, n_expert)
        def _(j):
            d = peer(j)
            p.w_stage[d] = p.w_one[source_of[d]]
            remote(
                p.w_stage.at[d], p.w_two.at[me], p.w_two_send.at[d], p.w_two_recv.at[me], (dp, d)
            ).start()

        p.w_two[me] = p.w_one[source_of[me]]

    def hop_first(p, part):
        pair_copy(p).wait_recv()

        def piece(i):
            at = part.where(i)
            gradient = p.own[at] + p.pair_in[at].astype(jnp.float32)
            after = adam_moments(p.mean[at], p.square[at], gradient)
            for k in range(2):
                p.stage[i, k] = after[k]

        @pl.loop(1, n_expert)
        def _(j):
            d = peer(j)
            piece(d)
            remote(
                p.stage.at[d], p.hop_one.at[me], p.one_send.at[d], p.one_recv.at[me], (dp, d)
            ).start()

        piece(me)
        p.hop_one[me] = p.stage[me]

    def hop_second(p, part):
        all_wait(p.stage, p.hop_one, p.one_send, p.one_recv, True)
        all_wait(p.stage, p.hop_one, p.one_send, p.one_recv, False)

        @pl.loop(1, n_expert)
        def _(j):
            d = peer(j)
            p.stage[d] = p.hop_one[source_of[d]]
            remote(
                p.stage.at[d], p.hop_two.at[me], p.two_send.at[d], p.two_recv.at[me], (dp, d)
            ).start()

        p.hop_two[me] = p.hop_one[source_of[me]]

    def arrive(p, part, results):
        all_wait(p.stage, p.hop_two, p.two_send, p.two_recv, False)
        all_wait(p.w_stage, p.w_two, p.w_two_send, p.w_two_recv, False)

        @pl.loop(0, n_expert)
        def _(i):
            at = part.where(i)
            for k in range(2):
                results[1 + k][at] = p.hop_two[i, k]
            results[0][at] = adam_weight(p.w_two[i], p.hop_two[i, 0], p.hop_two[i, 1])

    load(0).wait()
    z_first(tok)
    y_send(tok, zl)
    load(1).wait()
    y_send(cot, zl)
    z_step(tok, 0)
    z_first(cot)
    y_step(tok, 0)

    @pl.loop(1, n_line - 1)
    def _(step):
        z_step(tok, step)
        y_step(tok, step)

    z_step(cot, 0)
    y_step(cot, 0)
    for k in range(2, 8):
        load(k).wait()
    forward()
    z_step(cot, 1)
    w_first(pin, part_in)
    w_first(pout, part_out)
    y_step(cot, 1)
    turn()
    z_step(cot, 2)
    back_all("start")
    y_step(cot, 2)
    y_all(cot, False)
    ring_first(pout, part_out, sc.hid_t, lambda: cot.came[...].reshape(slots, width))
    backward()
    ring_second(pout, part_out)
    ring_first(pin, part_in, sc.tok_t, lambda: sc.slope[...])
    w_second(pin, part_in)
    w_second(pout, part_out)
    ring_third(pout, part_out)
    ring_second(pin, part_in)
    hop_first(pout, part_out)
    ring_third(pin, part_in)
    hop_first(pin, part_in)
    hop_second(pout, part_out)
    hop_second(pin, part_in)
    mix()
    arrive(pout, part_out, outs[4:7])
    arrive(pin, part_in, outs[1:4])
    z_sent(cot)
    y_all(cot, True)
    back_all("sent")
    z_sent(tok)
    for p, part in ((pout, part_out), (pin, part_in)):
        for k in range(6):
            ring_copies(p, part)(k).wait_send()
        pair_copy(p).wait_send()
        all_wait(p.stage, p.hop_two, p.two_send, p.two_recv, True)
        w_sent(p, part)
        all_wait(p.w_stage, p.w_two, p.w_two_send, p.w_two_recv, True)


def store_kernel(*refs):
    n = (len(refs) - 1) // 3
    sources, targets, held = refs[:n], refs[n : 2 * n], refs[2 * n : 3 * n]
    sem = refs[3 * n]
    fetch = [pltpu.make_async_copy(sources[k], held[k], sem.at[k]) for k in range(n)]
    put = [pltpu.make_async_copy(held[k], targets[k], sem.at[n + k]) for k in range(n)]
    for copy in fetch:
        copy.start()
    for k in range(n):
        fetch[k].wait()
        put[k].start()
    for copy in put:
        copy.wait()


def body(
    tokens,
    route_ids,
    route_gates,
    cotangent,
    old_owner,
    new_owner,
    weight_in,
    weight_out,
    mean_in,
    square_in,
    mean_out,
    square_out,
):
    n_expert = lax.axis_size("expert")
    n_groups = lax.axis_size("dp")
    tok_rows, width = tokens.shape
    picks_each = route_ids.shape[1]
    hidden_width = weight_in.shape[2]
    capacity = 2 * tok_rows * picks_each // n_expert
    rows_in = width // n_groups
    rows_out = hidden_width // n_groups
    experts_all = jnp.arange(n_expert, dtype=jnp.int32)
    holder = (new_owner[:, None] == experts_all[None, :]).astype(jnp.int32)
    source_of = jnp.sum(holder * old_owner[:, None], axis=0)
    parts = (
        Part(width, hidden_width, (16, hidden_width // 2)),
        Part(hidden_width, width, (rows_out // 2, 128)),
    )
    vmem = pl.BlockSpec(memory_space=pltpu.VMEM)
    smem = pl.BlockSpec(memory_space=pltpu.SMEM)
    far = pl.BlockSpec(memory_space=pl.ANY)
    shares_in = jax.ShapeDtypeStruct((rows_in, hidden_width), jnp.bfloat16)
    shares_out = jax.ShapeDtypeStruct((rows_out, width), jnp.bfloat16)
    flow = list(flow_scratch(tok_rows, capacity, width).values())
    other = other_scratch(tok_rows, capacity, width, hidden_width, n_expert)
    results = pl.pallas_call(
        functools.partial(whole_kernel, n_expert, parts),
        out_shape=[jax.ShapeDtypeStruct((tok_rows, width), jnp.bfloat16)]
        + [shares_in] * 3
        + [shares_out] * 3,
        in_specs=[smem] + [vmem] * 3 + [far] * 8,
        out_specs=[vmem] * 7,
        scratch_shapes=flow
        + flow
        + list(other.values())
        + list(parts[0].scratch(n_expert).values())
        + list(parts[1].scratch(n_expert).values()),
        compiler_params=pltpu.CompilerParams(
            collective_id=0, has_side_effects=True, vmem_limit_bytes=63 << 20
        ),
        name="whole",
    )(
        source_of,
        old_owner.reshape(1, n_expert),
        route_ids.T,
        route_gates.T,
        tokens,
        cotangent,
        weight_in[0],
        mean_in[0],
        square_in[0],
        weight_out[0],
        mean_out[0],
        square_out[0],
    )
    results = pl.pallas_call(
        store_kernel,
        out_shape=[jax.ShapeDtypeStruct(piece.shape, piece.dtype) for piece in results],
        in_specs=[far] * 7,
        out_specs=[far] * 7,
        scratch_shapes=[pltpu.VMEM(piece.shape, piece.dtype) for piece in results]
        + [pltpu.SemaphoreType.DMA((14,))],
        name="store",
    )(*results)
    return (results[0],) + tuple(piece[None] for piece in results[1:])


def solution(mesh):
    return jax.shard_map(
        body,
        mesh=mesh,
        in_specs=(
            P(("dp", "expert"), None),
            P(("dp", "expert"), None),
            P(("dp", "expert"), None),
            P(("dp", "expert"), None),
            P(),
            P(),
            P("expert", None, None),
            P("expert", None, None),
            P("expert", "dp", None),
            P("expert", "dp", None),
            P("expert", "dp", None),
            P("expert", "dp", None),
        ),
        out_specs=(
            P(("dp", "expert"), None),
            P("expert", "dp", None),
            P("expert", "dp", None),
            P("expert", "dp", None),
            P("expert", "dp", None),
            P("expert", "dp", None),
            P("expert", "dp", None),
        ),
        check_vma=False,
    )
```

```python
import functools

import jax
import jax.numpy as jnp
from jax import lax
from jax.experimental import pallas as pl
from jax.experimental.pallas import tpu as pltpu
from jax.sharding import PartitionSpec as P

beta_one = 0.9
beta_two = 0.95
adam_eps = 1e-08
learn_rate = 0.01
adam_step = 100.0
n_ring = 4
n_half = 2
MESH = pl.DeviceIdType.MESH


def silu_slope(preact):
    logistic = jax.nn.sigmoid(preact)
    return logistic * (1.0 + preact * (1.0 - logistic))


def adam_moments(mean_old, square_old, gradient):
    mean_new = beta_one * mean_old.astype(jnp.float32) + (1.0 - beta_one) * gradient
    square_new = beta_two * square_old.astype(jnp.float32) + (1.0 - beta_two) * gradient * gradient
    return mean_new.astype(jnp.bfloat16), square_new.astype(jnp.bfloat16)


def adam_weight(weight, mean_new, square_new):
    stride = (
        mean_new.astype(jnp.float32)
        / (1.0 - beta_one**adam_step)
        / (jnp.sqrt(square_new.astype(jnp.float32) / (1.0 - beta_two**adam_step)) + adam_eps)
    )
    return (weight.astype(jnp.float32) - learn_rate * stride).astype(jnp.bfloat16)


def outer_dot(left, right):
    return lax.dot_general(
        left, right, (((0,), (0,)), ((), ())), preferred_element_type=jnp.float32
    )


def right_dot(left, right):
    return lax.dot_general(
        left, right, (((1,), (1,)), ((), ())), preferred_element_type=jnp.float32
    )


def remote(src, dst, send, recv, device):
    return pltpu.make_async_remote_copy(
        src_ref=src, dst_ref=dst, send_sem=send, recv_sem=recv, device_id=device, device_id_type=MESH
    )


class Part:
    def __init__(self, rows, cols, piece):
        self.rows, self.cols, self.piece = rows, cols, piece
        self.share = rows // (n_ring * n_half)
        self.block = rows // n_ring
        self.side = cols // 2
        self.per_row = cols // piece[1]

    def where(self, i):
        r = pl.multiple_of((i // self.per_row) * self.piece[0], 16)
        c = pl.multiple_of((i % self.per_row) * self.piece[1], 128)
        return pl.ds(r, self.piece[0]), pl.ds(c, self.piece[1])

    def scratch(self, n_expert):
        half = (self.block, self.side)
        return dict(
            partial=pltpu.VMEM((self.rows, self.cols), jnp.bfloat16),
            landing=pltpu.VMEM((6,) + half, jnp.bfloat16),
            relayed=pltpu.VMEM((2,) + half, jnp.bfloat16),
            own=pltpu.VMEM((self.share, self.cols), jnp.float32),
            pair_out=pltpu.VMEM((self.share, self.cols), jnp.bfloat16),
            pair_in=pltpu.VMEM((self.share, self.cols), jnp.bfloat16),
            stage=pltpu.VMEM((n_expert, 2) + self.piece, jnp.bfloat16),
            hop_one=pltpu.VMEM((n_expert, 2) + self.piece, jnp.bfloat16),
            hop_two=pltpu.VMEM((n_expert, 2) + self.piece, jnp.bfloat16),
            w_one=pltpu.VMEM((n_expert,) + self.piece, jnp.bfloat16),
            w_stage=pltpu.VMEM((n_expert,) + self.piece, jnp.bfloat16),
            w_two=pltpu.VMEM((n_expert,) + self.piece, jnp.bfloat16),
            w_one_send=pltpu.SemaphoreType.DMA((n_expert,)),
            w_one_recv=pltpu.SemaphoreType.DMA((n_expert,)),
            w_two_send=pltpu.SemaphoreType.DMA((n_expert,)),
            w_two_recv=pltpu.SemaphoreType.DMA((n_expert,)),
            weight=pltpu.VMEM((self.rows, self.cols), jnp.bfloat16),
            mean=pltpu.VMEM((self.share, self.cols), jnp.bfloat16),
            square=pltpu.VMEM((self.share, self.cols), jnp.bfloat16),
            load=pltpu.SemaphoreType.DMA((3,)),
            ring_send=pltpu.SemaphoreType.DMA((6,)),
            ring_recv=pltpu.SemaphoreType.DMA((6,)),
            pair_send=pltpu.SemaphoreType.DMA,
            pair_recv=pltpu.SemaphoreType.DMA,
            one_send=pltpu.SemaphoreType.DMA((n_expert,)),
            one_recv=pltpu.SemaphoreType.DMA((n_expert,)),
            two_send=pltpu.SemaphoreType.DMA((n_expert,)),
            two_recv=pltpu.SemaphoreType.DMA((n_expert,)),
        )


part_names = tuple(Part(128, 256, (16, 128)).scratch(32))
n_line = 4
n_plane = 8


def flow_scratch(rows, cap, width):
    return dict(
        raw=pltpu.VMEM((n_line, rows, width), jnp.bfloat16),
        sent=pltpu.VMEM((n_line, n_plane, cap, width), jnp.bfloat16),
        came=pltpu.VMEM((n_line, n_plane, cap, width), jnp.bfloat16),
        load=pltpu.SemaphoreType.DMA,
        z_send=pltpu.SemaphoreType.DMA((2, n_line)),
        z_recv=pltpu.SemaphoreType.DMA((n_line,)),
        y_send=pltpu.SemaphoreType.DMA((n_line, n_plane)),
        y_recv=pltpu.SemaphoreType.DMA((n_line, n_plane)),
    )


flow_names = tuple(flow_scratch(128, 16, 2048))


def other_scratch(rows, cap, width, hidden, n_expert):
    slots = n_expert * cap
    return dict(
        meta=pltpu.VMEM((n_line, 8, rows), jnp.float32),
        meta_send=pltpu.SemaphoreType.DMA((2, n_line)),
        meta_recv=pltpu.SemaphoreType.DMA((n_line,)),
        preact=pltpu.VMEM((slots, hidden), jnp.float32),
        hid_t=pltpu.VMEM((hidden, slots), jnp.bfloat16),
        tok_t=pltpu.VMEM((width, slots), jnp.bfloat16),
        slope=pltpu.VMEM((slots, hidden), jnp.bfloat16),
        returned=pltpu.VMEM((n_expert, cap, width), jnp.bfloat16),
        back_send=pltpu.SemaphoreType.DMA((n_expert,)),
        back_recv=pltpu.SemaphoreType.DMA((n_expert,)),
    )


other_names = tuple(other_scratch(128, 16, 2048, 768, 32))


class Refs:
    def __init__(self, names, refs):
        for name, ref in zip(names, refs):
            setattr(self, name, ref)


def whole_kernel(n_expert, parts, *refs):
    (
        source_of,
        owner,
        route_ids,
        gates,
        tokens,
        cotangent,
        w_in,
        m_in,
        s_in,
        w_out,
        m_out,
        s_out,
    ) = refs[:12]
    outs = refs[12:19]
    mixed = outs[0]
    rest = list(refs[19:])

    def take(names):
        group = Refs(names, rest[: len(names)])
        del rest[: len(names)]
        return group

    tok, cot = take(flow_names), take(flow_names)
    sc = take(other_names)
    pin, pout = take(part_names), take(part_names)
    part_in, part_out = parts
    rows, width = mixed.shape
    cap = sc.returned.shape[1]
    slots = n_expert * cap
    dp = lax.axis_index("dp")
    me = lax.axis_index("expert")
    x, zh = dp // 2, dp % 2
    ahead, behind, across = (x + 1) % 4, (x + 3) % 4, (x + 2) % 4
    to_ahead = (ahead * 2 + zh, me)
    to_behind = (behind * 2 + zh, me)
    to_pair = (x * 2 + 1 - zh, me)
    peers = n_expert - 1
    zl = (me // 2) % n_line
    mine = (me // 8) * 2 + me % 2

    def peer(j):
        return (me + j) % n_expert

    def other_half(i):
        apart = (i // 2) % n_line - zl
        return (
            (apart == 3)
            | (apart == -3)
            | (((apart == 2) | (apart == -2)) & (i % 2 == me % 2))
        )

    def loads():
        plan = [
            (tokens, tok.raw.at[zl], tok.load),
            (cotangent, cot.raw.at[zl], cot.load),
        ]
        for p, sources in ((pin, (w_in, m_in, s_in)), (pout, (w_out, m_out, s_out))):
            for k, target in enumerate((p.weight, p.mean, p.square)):
                plan.append((sources[k], target, p.load.at[k]))
        return plan

    def load(k):
        return pltpu.make_async_copy(*loads()[k])

    for k in range(8):
        load(k).start()

    barrier = pltpu.get_barrier_semaphore()

    @pl.loop(1, n_expert)
    def _(j):
        pl.semaphore_signal(barrier, inc=1, device_id=(dp, peer(j)), device_id_type=MESH)

    for device in (to_ahead, to_behind, to_pair):
        pl.semaphore_signal(barrier, inc=1, device_id=device, device_id_type=MESH)

    @pl.loop(0, n_expert)
    def _(i):
        @pl.when(other_half(i))
        def _():
            pl.semaphore_signal(
                barrier, inc=1, device_id=(x * 2 + 1 - zh, i), device_id_type=MESH
            )


    def place_own():
        def column(ref, k):
            return jnp.broadcast_to(ref[k : k + 1, :].astype(jnp.float32), (rows, rows)).T

        lanes = lax.broadcasted_iota(jnp.int32, (rows, n_expert), 1).astype(jnp.float32)
        picked = [(column(route_ids, k)[:, 0:1] == lanes).astype(jnp.float32) for k in range(2)]
        earlier = (
            lax.broadcasted_iota(jnp.int32, (rows, rows), 1)
            < lax.broadcasted_iota(jnp.int32, (rows, rows), 0)
        ).astype(jnp.float32)
        before = jnp.dot(
            earlier.astype(jnp.bfloat16),
            (picked[0] + picked[1]).astype(jnp.bfloat16),
            preferred_element_type=jnp.float32,
        )
        held = owner[...].astype(jnp.float32) * float(cap)
        slot = [jnp.sum(one * (before + held), axis=1, keepdims=True) for one in picked]
        lane = lax.broadcasted_iota(jnp.int32, (rows, 128), 1)
        table = jnp.where(
            lane == 0,
            slot[0],
            jnp.where(lane == 1, slot[1], jnp.where(lane == 2, column(gates, 0), column(gates, 1))),
        )
        sc.meta[zl] = table.T[0:8, :]

    place_own()
    far_half = jnp.where((zl == 0) | (zl == n_line - 1), 12, 4)
    pl.semaphore_wait(barrier, peers + 3 + far_half)

    def z_copies(buf, send, recv, direction, block):
        neighbour = (dp, me + 2 if direction == 0 else me - 2)
        return remote(
            buf.at[block], buf.at[block], send.at[direction, block], recv.at[block], neighbour
        )

    def z_send(flow, direction, block):
        z_copies(flow.raw, flow.z_send, flow.z_recv, direction, block).start()
        if flow is tok:
            z_copies(sc.meta, sc.meta_send, sc.meta_recv, direction, block).start()

    def z_wait(flow, direction, block, sent):
        copy = z_copies(flow.raw, flow.z_send, flow.z_recv, direction, block)
        copy.wait_send() if sent else copy.wait_recv()
        if flow is tok:
            copy = z_copies(sc.meta, sc.meta_send, sc.meta_recv, direction, block)
            copy.wait_send() if sent else copy.wait_recv()

    def z_first(flow):
        pl.when(zl < n_line - 1)(lambda: z_send(flow, 0, zl))
        pl.when(zl > 0)(lambda: z_send(flow, 1, zl))

    def z_step(flow, step):
        left, right = zl - 1 - step, zl + 1 + step

        @pl.when(left >= 0)
        def _():
            z_wait(flow, 0, left, False)
            pl.when(zl < n_line - 1)(lambda: z_send(flow, 0, left))

        @pl.when(right < n_line)
        def _():
            z_wait(flow, 1, right, False)
            pl.when(zl > 0)(lambda: z_send(flow, 1, right))

    def z_sent(flow):
        @pl.loop(0, n_line)
        def _(block):
            pl.when((zl < n_line - 1) & (block <= zl))(lambda: z_wait(flow, 0, block, True))
            pl.when((zl > 0) & (block >= zl))(lambda: z_wait(flow, 1, block, True))

    def y_copy(flow, block, q):
        device = (dp, (q // 2) * 8 + zl * 2 + q % 2)
        return remote(
            flow.sent.at[block, q],
            flow.came.at[block, mine],
            flow.y_send.at[block, q],
            flow.y_recv.at[block, mine],
            device,
        )

    def y_got(flow, block, q):
        device = (dp, (q // 2) * 8 + zl * 2 + q % 2)
        return remote(
            flow.sent.at[block, q],
            flow.came.at[block, q],
            flow.y_send.at[block, q],
            flow.y_recv.at[block, q],
            device,
        )

    def y_send(flow, block):
        r = lax.broadcasted_iota(jnp.int32, (n_plane * cap, rows), 0)
        here = ((r // (2 * cap)) * (n_expert * cap // 4) + r % (2 * cap) + zl * (2 * cap)).astype(
            jnp.float32
        )
        pick = [
            (sc.meta[block, k : k + 1, :] == here).astype(jnp.float32).astype(jnp.bfloat16)
            for k in range(2)
        ]
        if flow is tok:
            put = jnp.dot(pick[0] + pick[1], flow.raw[block], preferred_element_type=jnp.float32)
        else:
            put = None
            for k in range(2):
                gate = jnp.broadcast_to(sc.meta[block, 2 + k : 3 + k, :], (rows, rows)).T[:, 0:1]
                scaled = (gate * flow.raw[block].astype(jnp.float32)).astype(jnp.bfloat16)
                term = jnp.dot(pick[k], scaled, preferred_element_type=jnp.float32)
                put = term if put is None else put + term
        flow.sent[block] = put.astype(jnp.bfloat16).reshape(n_plane, cap, width)

        @pl.loop(1, n_plane)
        def _(j):
            y_copy(flow, block, (mine + j) % n_plane).start()

        flow.came[block, mine] = flow.sent[block, mine]

    def y_step(flow, step):
        left, right = zl - 1 - step, zl + 1 + step
        pl.when(left >= 0)(lambda: y_send(flow, left))
        pl.when(right < n_line)(lambda: y_send(flow, right))

    def y_all(flow, sent):
        @pl.loop(0, n_line)
        def _(block):
            @pl.loop(1, n_plane)
            def _(j):
                q = (mine + j) % n_plane
                if sent:
                    y_copy(flow, block, q).wait_send()
                else:
                    y_got(flow, block, q).wait_recv()

    def forward():
        y_all(tok, False)
        y_all(tok, True)
        step = n_plane * cap

        @pl.loop(0, n_line)
        def _(i):
            r = pl.ds(pl.multiple_of(i * step, step), step)
            preact = jnp.dot(
                tok.came[i].reshape(step, width), pin.weight[...], preferred_element_type=jnp.float32
            )
            sc.preact[r, :] = preact
            hidden = jax.nn.silu(preact).astype(jnp.bfloat16)
            tok.sent[i] = (
                jnp.dot(hidden, pout.weight[...], preferred_element_type=jnp.float32)
                .astype(jnp.bfloat16)
                .reshape(n_plane, cap, width)
            )
            sc.hid_t[:, r] = hidden.T

    def turn():
        step = n_plane * cap

        @pl.loop(0, n_line)
        def _(i):
            r = pl.ds(pl.multiple_of(i * step, step), step)
            sc.tok_t[:, r] = tok.came[i].reshape(step, width).T

    def backward():
        step = n_plane * cap

        @pl.loop(0, n_line)
        def _(i):
            r = pl.ds(pl.multiple_of(i * step, step), step)
            downward = right_dot(cot.came[i].reshape(step, width), pout.weight[...])
            sc.slope[r, :] = (downward * silu_slope(sc.preact[r, :])).astype(jnp.bfloat16)

    def back_copy(d, landing):
        block, q = (d // 2) % n_line, (d // 8) * 2 + d % 2
        return remote(
            tok.sent.at[block, q],
            sc.returned.at[landing],
            sc.back_send.at[d],
            sc.back_recv.at[landing],
            (dp, d),
        )

    def back_all(what):
        @pl.loop(1, n_expert)
        def _(j):
            d = peer(j)
            if what == "start":
                back_copy(d, me).start()
            elif what == "recv":
                back_copy(d, d).wait_recv()
            else:
                back_copy(d, me).wait_send()

        if what == "start":
            sc.returned[me] = tok.sent[zl, mine]

    def mix():
        back_all("recv")
        back = sc.returned[...].reshape(slots, width)
        lanes = lax.broadcasted_iota(jnp.int32, (rows, slots), 1).astype(jnp.float32)
        total = None
        for k in range(2):
            slot = jnp.broadcast_to(sc.meta[zl, k : k + 1, :], (rows, rows)).T[:, 0:1]
            gate = jnp.broadcast_to(sc.meta[zl, 2 + k : 3 + k, :], (rows, rows)).T[:, 0:1]
            pick = (slot == lanes).astype(jnp.float32).astype(jnp.bfloat16)
            term = gate * jnp.dot(pick, back, preferred_element_type=jnp.float32)
            total = term if total is None else total + term
        mixed[...] = total.astype(jnp.bfloat16)

    def all_wait(src, dst, send, recv, sent):
        @pl.loop(1, n_expert)
        def _(j):
            d = peer(j)
            copy = remote(src.at[d], dst.at[d], send.at[d], recv.at[d], (dp, d))
            copy.wait_send() if sent else copy.wait_recv()

    def ring_copies(p, part):
        def side(block, half):
            r = pl.multiple_of(block * part.block, 16)
            return p.partial.at[pl.ds(r, part.block), pl.ds(half * part.side, part.side)]

        plan = [
            (side(across, 0), 0, to_ahead),
            (side(across, 1), 1, to_behind),
            (side(ahead, 1), 2, to_ahead),
            (side(behind, 0), 3, to_behind),
            (p.relayed.at[0], 4, to_ahead),
            (p.relayed.at[1], 5, to_behind),
        ]
        def copy(k):
            src, slot_of, device = plan[k]
            return remote(
                src, p.landing.at[slot_of], p.ring_send.at[k], p.ring_recv.at[k], device
            )

        return copy

    def ring_first(p, part, left, right):
        def fill(block):
            step = min(part.block, 256)
            base = block * part.block

            @pl.loop(0, part.block // step)
            def _(i):
                r = pl.ds(pl.multiple_of(base + i * step, 16), step)
                p.partial[r, :] = jnp.dot(
                    left[r, :], right(), preferred_element_type=jnp.float32
                ).astype(jnp.bfloat16)

        copies = ring_copies(p, part)
        fill(across)
        copies(0).start()
        copies(1).start()
        fill(ahead)
        copies(2).start()
        fill(behind)
        copies(3).start()
        fill(x)

    def ring_second(p, part):
        copies = ring_copies(p, part)
        for k, block in ((0, ahead), (1, behind)):
            copies(k).wait_recv()

            @pl.loop(0, part.block // 16)
            def _(i):
                r = pl.ds(pl.multiple_of(i * 16, 16), 16)
                q = pl.ds(pl.multiple_of(block * part.block + i * 16, 16), 16)
                mine = p.partial[q, pl.ds(k * part.side, part.side)].astype(jnp.float32)
                p.relayed[k, r, :] = (p.landing[k, r, :].astype(jnp.float32) + mine).astype(
                    jnp.bfloat16
                )

            copies(4 + k).start()

    def pair_copy(p):
        return remote(p.pair_out, p.pair_in, p.pair_send, p.pair_recv, to_pair)

    def ring_third(p, part):
        copies = ring_copies(p, part)
        for k in (2, 3, 4, 5):
            copies(k).wait_recv()

        def total(half, base, i, k):
            r = pl.ds(pl.multiple_of(base + i * 16, 16), 16)
            q = pl.ds(pl.multiple_of(x * part.block + base + i * 16, 16), 16)
            mine = p.partial[q, pl.ds(half * part.side, part.side)].astype(jnp.float32)
            return (
                mine
                + p.landing[4 + half, r, :].astype(jnp.float32)
                + p.landing[3 - half, r, :].astype(jnp.float32)
            )

        @pl.loop(0, part.share // 16)
        def _(i):
            q = pl.ds(pl.multiple_of(i * 16, 16), 16)
            for half in range(2):
                p.pair_out[q, pl.ds(half * part.side, part.side)] = total(
                    half, (1 - zh) * part.share, i, 0
                ).astype(jnp.bfloat16)

        pair_copy(p).start()

        @pl.loop(0, part.share // 16)
        def _(i):
            q = pl.ds(pl.multiple_of(i * 16, 16), 16)
            for half in range(2):
                p.own[q, pl.ds(half * part.side, part.side)] = total(half, zh * part.share, i, 0)

    def w_copy(p, part, i):
        to = x * 2 + jnp.where(other_half(i), 1 - zh, zh)
        at = part.where(i)
        r = (i // part.per_row) * part.piece[0] + to * part.share
        source = p.weight.at[pl.ds(pl.multiple_of(r, 16), part.piece[0]), at[1]]
        return remote(source, p.w_one.at[me], p.w_one_send.at[i], p.w_one_recv.at[me], (to, i))

    def w_first(p, part):
        @pl.loop(1, n_expert)
        def _(j):
            w_copy(p, part, peer(j)).start()

        at = part.where(me)
        r = (me // part.per_row) * part.piece[0] + dp * part.share
        p.w_one[me] = p.weight[pl.ds(pl.multiple_of(r, 16), part.piece[0]), at[1]]

    def w_sent(p, part):
        @pl.loop(1, n_expert)
        def _(j):
            w_copy(p, part, peer(j)).wait_send()

    def w_second(p, part):
        all_wait(p.w_stage, p.w_one, p.w_one_send, p.w_one_recv, False)

        @pl.loop(1, n_expert)
        def _(j):
            d = peer(j)
            p.w_stage[d] = p.w_one[source_of[d]]
            remote(
                p.w_stage.at[d], p.w_two.at[me], p.w_two_send.at[d], p.w_two_recv.at[me], (dp, d)
            ).start()

        p.w_two[me] = p.w_one[source_of[me]]

    def hop_first(p, part):
        pair_copy(p).wait_recv()

        def piece(i):
            at = part.where(i)
            gradient = p.own[at] + p.pair_in[at].astype(jnp.float32)
            after = adam_moments(p.mean[at], p.square[at], gradient)
            for k in range(2):
                p.stage[i, k] = after[k]

        @pl.loop(1, n_expert)
        def _(j):
            d = peer(j)
            piece(d)
            remote(
                p.stage.at[d], p.hop_one.at[me], p.one_send.at[d], p.one_recv.at[me], (dp, d)
            ).start()

        piece(me)
        p.hop_one[me] = p.stage[me]

    def hop_second(p, part):
        all_wait(p.stage, p.hop_one, p.one_send, p.one_recv, True)
        all_wait(p.stage, p.hop_one, p.one_send, p.one_recv, False)

        @pl.loop(1, n_expert)
        def _(j):
            d = peer(j)
            p.stage[d] = p.hop_one[source_of[d]]
            remote(
                p.stage.at[d], p.hop_two.at[me], p.two_send.at[d], p.two_recv.at[me], (dp, d)
            ).start()

        p.hop_two[me] = p.hop_one[source_of[me]]

    def arrive(p, part, results):
        all_wait(p.w_stage, p.w_two, p.w_two_send, p.w_two_recv, False)

        def piece(i):
            at = part.where(i)
            for k in range(2):
                results[1 + k][at] = p.hop_two[i, k]
            results[0][at] = adam_weight(p.w_two[i], p.hop_two[i, 0], p.hop_two[i, 1])

        piece(me)

        @pl.loop(1, n_expert)
        def _(j):
            d = peer(j)
            copy = remote(
                p.stage.at[d], p.hop_two.at[d], p.two_send.at[d], p.two_recv.at[d], (dp, d)
            )
            copy.wait_recv()
            piece(d)

    load(0).wait()
    z_first(tok)
    y_send(tok, zl)
    load(1).wait()
    y_send(cot, zl)
    z_step(tok, 0)
    z_first(cot)
    y_step(tok, 0)

    @pl.loop(1, n_line - 1)
    def _(step):
        z_step(tok, step)
        y_step(tok, step)

    z_step(cot, 0)
    y_step(cot, 0)
    for k in range(2, 8):
        load(k).wait()
    forward()
    z_step(cot, 1)
    w_first(pin, part_in)
    w_first(pout, part_out)
    y_step(cot, 1)
    back_all("start")
    turn()
    z_step(cot, 2)
    y_step(cot, 2)
    y_all(cot, False)
    ring_first(pout, part_out, sc.hid_t, lambda: cot.came[...].reshape(slots, width))
    backward()
    ring_second(pout, part_out)
    w_second(pin, part_in)
    w_second(pout, part_out)
    ring_first(pin, part_in, sc.tok_t, lambda: sc.slope[...])
    ring_third(pout, part_out)
    ring_second(pin, part_in)
    hop_first(pout, part_out)
    ring_third(pin, part_in)
    hop_first(pin, part_in)
    hop_second(pout, part_out)
    hop_second(pin, part_in)
    mix()
    arrive(pout, part_out, outs[4:7])
    arrive(pin, part_in, outs[1:4])
    z_sent(cot)
    y_all(cot, True)
    back_all("sent")
    z_sent(tok)
    for p, part in ((pout, part_out), (pin, part_in)):
        for k in range(6):
            ring_copies(p, part)(k).wait_send()
        pair_copy(p).wait_send()
        all_wait(p.stage, p.hop_two, p.two_send, p.two_recv, True)
        w_sent(p, part)
        all_wait(p.w_stage, p.w_two, p.w_two_send, p.w_two_recv, True)


def store_kernel(*refs):
    n = (len(refs) - 1) // 3
    sources, targets, held = refs[:n], refs[n : 2 * n], refs[2 * n : 3 * n]
    sem = refs[3 * n]
    fetch = [pltpu.make_async_copy(sources[k], held[k], sem.at[k]) for k in range(n)]
    put = [pltpu.make_async_copy(held[k], targets[k], sem.at[n + k]) for k in range(n)]
    for copy in fetch:
        copy.start()
    for k in range(n):
        fetch[k].wait()
        put[k].start()
    for copy in put:
        copy.wait()


def body(
    tokens,
    route_ids,
    route_gates,
    cotangent,
    old_owner,
    new_owner,
    weight_in,
    weight_out,
    mean_in,
    square_in,
    mean_out,
    square_out,
):
    n_expert = lax.axis_size("expert")
    n_groups = lax.axis_size("dp")
    tok_rows, width = tokens.shape
    picks_each = route_ids.shape[1]
    hidden_width = weight_in.shape[2]
    capacity = 2 * tok_rows * picks_each // n_expert
    rows_in = width // n_groups
    rows_out = hidden_width // n_groups
    experts_all = jnp.arange(n_expert, dtype=jnp.int32)
    holder = (new_owner[:, None] == experts_all[None, :]).astype(jnp.int32)
    source_of = jnp.sum(holder * old_owner[:, None], axis=0)
    parts = (
        Part(width, hidden_width, (16, hidden_width // 2)),
        Part(hidden_width, width, (rows_out // 2, 128)),
    )
    vmem = pl.BlockSpec(memory_space=pltpu.VMEM)
    smem = pl.BlockSpec(memory_space=pltpu.SMEM)
    far = pl.BlockSpec(memory_space=pl.ANY)
    shares_in = jax.ShapeDtypeStruct((rows_in, hidden_width), jnp.bfloat16)
    shares_out = jax.ShapeDtypeStruct((rows_out, width), jnp.bfloat16)
    flow = list(flow_scratch(tok_rows, capacity, width).values())
    other = other_scratch(tok_rows, capacity, width, hidden_width, n_expert)
    results = pl.pallas_call(
        functools.partial(whole_kernel, n_expert, parts),
        out_shape=[jax.ShapeDtypeStruct((tok_rows, width), jnp.bfloat16)]
        + [shares_in] * 3
        + [shares_out] * 3,
        in_specs=[smem] + [vmem] * 3 + [far] * 8,
        out_specs=[vmem] * 7,
        scratch_shapes=flow
        + flow
        + list(other.values())
        + list(parts[0].scratch(n_expert).values())
        + list(parts[1].scratch(n_expert).values()),
        compiler_params=pltpu.CompilerParams(
            collective_id=0, has_side_effects=True, vmem_limit_bytes=63 << 20
        ),
        name="whole",
    )(
        source_of,
        old_owner.reshape(1, n_expert),
        route_ids.T,
        route_gates.T,
        tokens,
        cotangent,
        weight_in[0],
        mean_in[0],
        square_in[0],
        weight_out[0],
        mean_out[0],
        square_out[0],
    )
    results = pl.pallas_call(
        store_kernel,
        out_shape=[jax.ShapeDtypeStruct(piece.shape, piece.dtype) for piece in results],
        in_specs=[far] * 7,
        out_specs=[far] * 7,
        scratch_shapes=[pltpu.VMEM(piece.shape, piece.dtype) for piece in results]
        + [pltpu.SemaphoreType.DMA((14,))],
        name="store",
    )(*results)
    return (results[0],) + tuple(piece[None] for piece in results[1:])


def solution(mesh):
    return jax.shard_map(
        body,
        mesh=mesh,
        in_specs=(
            P(("dp", "expert"), None),
            P(("dp", "expert"), None),
            P(("dp", "expert"), None),
            P(("dp", "expert"), None),
            P(),
            P(),
            P("expert", None, None),
            P("expert", None, None),
            P("expert", "dp", None),
            P("expert", "dp", None),
            P("expert", "dp", None),
            P("expert", "dp", None),
        ),
        out_specs=(
            P(("dp", "expert"), None),
            P("expert", "dp", None),
            P("expert", "dp", None),
            P("expert", "dp", None),
            P("expert", "dp", None),
            P("expert", "dp", None),
            P("expert", "dp", None),
        ),
        check_vma=False,
    )
```
